32 devices in a mesh: dp: 4 (over y, x), row: 4 (over z), col: 2 (over core).
Axes of the slice: x: 2, y: 2, z: 4, core: 2. Of those that a mesh axis runs over, the one named last changes fastest.
Arguments:
- block_input: bfloat16 [16384, 1024], P(('dp', 'row', 'col')), may hold values from -6 to 6
- d_out: bfloat16 [16384, 1024], P(('dp', 'row', 'col')), may hold values from -6 to 6
- lengths: int32 [4, 6], P('dp'), may hold values from 0 to 2048, as said below
- gain_in: float32 [1024], replicated, may hold values from 0.5 to 1.5
- w_z: bfloat16 [1024, 2048], P(None, ('row', 'col')), may hold values from -0.1875 to 0.1875
- w_x: bfloat16 [1024, 2048], P(None, ('row', 'col')), may hold values from -0.1875 to 0.1875
- w_bc: bfloat16 [1024, 256], P(None, ('row', 'col')), may hold values from -0.1875 to 0.1875
- w_dt: bfloat16 [1024, 32], P(None, ('row', 'col')), may hold values from -0.1875 to 0.1875
- conv_x: float32 [4, 2048], P(None, ('row', 'col')), may hold values from -3 to 3
- conv_x_bias: float32 [2048], P(('row', 'col')), may hold values from -0.5 to 0.5
- conv_bc: float32 [4, 256], P(None, ('row', 'col')), may hold values from -3 to 3
- conv_bc_bias: float32 [256], P(('row', 'col')), may hold values from -0.5 to 0.5
- dt_bias: float32 [32], P(('row', 'col')), may hold values from -6 to -2
- a_log: float32 [32], P(('row', 'col')), may hold values from -1.5 to 2.8
- d_skip: float32 [32], P(('row', 'col')), may hold values from 0.5 to 1.5
- gain_gate: float32 [2048], P(('row', 'col')), may hold values from 0.5 to 1.5
- w_out: bfloat16 [2048, 1024], P(('row', 'col')), may hold values from -0.125 to 0.125
Outputs:
- block_out: bfloat16 [16384, 1024], P(('dp', 'row', 'col'))
- d_x: float32 [16384, 1024], P(('dp', 'row', 'col'))
- d_gain_in: float32 [1024], replicated
- d_w_z: float32 [1024, 2048], P(None, ('row', 'col'))
- d_w_x: float32 [1024, 2048], P(None, ('row', 'col'))
- d_w_bc: float32 [1024, 256], P(None, ('row', 'col'))
- d_w_dt: float32 [1024, 32], P(None, ('row', 'col'))
- d_conv_x: float32 [4, 2048], P(None, ('row', 'col'))
- d_conv_x_bias: float32 [2048], P(('row', 'col'))
- d_conv_bc: float32 [4, 256], P(None, ('row', 'col'))
- d_conv_bc_bias: float32 [256], P(('row', 'col'))
- d_dt_bias: float32 [32], P(('row', 'col'))
- d_a_log: float32 [32], P(('row', 'col'))
- d_d_skip: float32 [32], P(('row', 'col'))
- d_gain_gate: float32 [2048], P(('row', 'col'))
- d_w_out: float32 [2048, 1024], P(('row', 'col'))
The draws below stay inside these ranges and needn't reach their ends.
Inputs may be any that keep to these rules, and one draw needn't show every extreme that they name: `lengths`: each row lists one replica's sequences in order from its first token slot; every entry is a multiple of 256; a row's entries sum to more than 2048 and at most 4096, the slots after that sum are padding; row 0 sums to 4096, and row 0 holds a sequence of 2048 tokens, the longest that a draw gives.
All inputs are finite; a program needn't handle non-finite values.
Results may differ from the reference program's by a relative error of at most 0.022.
Values may be sent and summed in bfloat16 or wider, within the bound.
No kernel may reach another device: no remote copies, remote signals or barrier semaphores. Data moves between devices by JAX's collectives and lax.ppermute only.
A program may use at most 192 MiB of HBM per device.

```python
from functools import partial
import jax
import jax.numpy as jnp
from jax import lax

D = 1024
H = 32
HEAD = 64
NS = 128
CONV = 4
BLOCK = 256
SEQ_MIN = 1024
SEQ_MAX = 4096
DI = 2048
TOK_REP = 4096
REPLICAS = 4
TOKENS = 16384
SEQS = 6
N_DP = 4


def draw_lengths(key, part):
    key = jax.random.fold_in(key, 7)
    cells = TOK_REP // BLOCK
    least = max(1, min(SEQ_MIN // BLOCK, cells // 4))
    most = max(least, min(SEQ_MAX // BLOCK, cells // 2))
    middle = cells // 2
    keys = jax.random.split(key, 4)
    first = jax.random.randint(keys[0], (REPLICAS,), least, min(most, middle - 1) + 1)
    floor_second = jnp.maximum(middle + 1 - first, least)
    second = jax.random.randint(keys[1], (REPLICAS,), floor_second, most + 1)
    second = second.at[0].set(most)
    others = jax.random.randint(keys[2], (REPLICAS, SEQS - 2), least, most + 1)
    spans = jnp.concatenate([first[:, None], second[:, None], others], axis=1)
    filled = jax.random.randint(keys[3], (REPLICAS,), middle + 1, cells + 1)
    filled = filled.at[0].set(cells)
    ends = jnp.cumsum(spans, axis=1)
    cut = jnp.clip(jnp.minimum(ends, filled[:, None]) - (ends - spans), 0, None)
    return (cut * BLOCK).astype(jnp.int32)


def levels(stream_key, shape, cuts, low, high):
    factor_of = 1.0
    for position, shards_of in cuts:
        heights = jax.random.uniform(jax.random.fold_in(jax.random.fold_in(stream_key, 6), position), (shards_of,), jnp.float32, low / len(cuts), high / len(cuts))
        factor_of = factor_of * jnp.repeat(jnp.exp(heights), shape[position] // shards_of).reshape((-1,) + (1,) * (len(shape) - 1 - position))
    return factor_of


def centred(key, extent, scale, most, cuts=(), kind=jnp.bfloat16):
    drawn = jax.random.normal(key, extent, jnp.float32) * scale
    if len(cuts) > 0:
        drawn = levels(key, extent, cuts, -0.22, 0.18) * drawn
    return jnp.clip(drawn, min=-most, max=most).astype(kind)


def setup_inputs(seed: int = 0) -> dict:
    splits = jax.random.split(jax.random.key(seed), 18)
    block_input = centred(splits[0], (TOKENS, D), 1.0, 6.0, ((0, 32),))
    d_out = centred(splits[1], (TOKENS, D), 1.0, 6.0, ((0, 32),))
    lengths = draw_lengths(jax.random.fold_in(splits[17], 71), 0)
    gain_in = jnp.clip(1.0 + 0.1 * jax.random.normal(splits[3], (D,), jnp.float32), 0.5, 1.5)
    w_z = centred(splits[4], (D, DI), D ** -0.5, 0.1875, ((1, 8),))
    w_x = centred(splits[5], (D, DI), D ** -0.5, 0.1875, ((1, 8),))
    w_bc = centred(splits[6], (D, 2 * NS), D ** -0.5, 0.1875, ((1, 8),))
    w_dt = centred(splits[7], (D, H), D ** -0.5, 0.1875, ((1, 8),))
    conv_x = centred(splits[8], (CONV, DI), CONV ** -0.5, 3.0, ((1, 8),), jnp.float32)
    conv_x_bias = jnp.clip(jax.random.uniform(splits[9], (DI,), jnp.float32, -0.5, 0.5) * levels(splits[9], (DI,), ((0, 8),), -0.4, 0.0), -0.5, 0.5)
    conv_bc = centred(splits[10], (CONV, 2 * NS), CONV ** -0.5, 3.0, ((1, 8),), jnp.float32)
    conv_bc_bias = jnp.clip(jax.random.uniform(splits[11], (2 * NS,), jnp.float32, -0.5, 0.5) * levels(splits[11], (2 * NS,), ((0, 8),), -0.4, 0.0), -0.5, 0.5)
    dt_bias = jnp.clip(-6.0 + 4.0 * jax.random.uniform(splits[12], (H,), jnp.float32) ** levels(splits[12], (H,), ((0, 8),), -0.2, 0.2), -6.0, -2.0)
    a_log = jnp.clip(-1.5 + 4.3 * jax.random.uniform(splits[13], (H,), jnp.float32) ** levels(splits[13], (H,), ((0, 8),), -0.2, 0.2), -1.5, 2.8)
    d_skip = jnp.clip(0.5 + 1.0 * jax.random.uniform(splits[14], (H,), jnp.float32) ** levels(splits[14], (H,), ((0, 8),), -0.2, 0.2), 0.5, 1.5)
    gain_gate = jnp.clip(1.0 + 0.1 * jax.random.normal(splits[15], (DI,), jnp.float32), 0.5, 1.5)
    w_out = centred(splits[16], (DI, D), DI ** -0.5, 0.125, ((0, 8),))
    return {"block_input": block_input, "d_out": d_out, "lengths": lengths, "gain_in": gain_in, "w_z": w_z, "w_x": w_x, "w_bc": w_bc, "w_dt": w_dt, "conv_x": conv_x, "conv_x_bias": conv_x_bias, "conv_bc": conv_bc, "conv_bc_bias": conv_bc_bias, "dt_bias": dt_bias, "a_log": a_log, "d_skip": d_skip, "gain_gate": gain_gate, "w_out": w_out}


@jax.custom_vjp
def low(v):
    return lax.optimization_barrier(v.astype(jnp.bfloat16)).astype(jnp.float32)

@jax.custom_vjp
def low_back(v):
    return v

def low_keep(v):
    return (low(v), None)

def low_pass(kept, grad):
    return (grad,)

def back_keep(v):
    return (v, None)

def back_low(kept, grad):
    return (low(grad),)
low.defvjp(low_keep, low_pass)
low_back.defvjp(back_keep, back_low)
epsilon = 1e-05
highest = lax.Precision.HIGHEST

def conv_silu(values, weight, bias, segment):
    summed = values * weight[CONV - 1] + bias
    for offset in range(1, CONV):
        shifted = jnp.concatenate([jnp.zeros((offset, values.shape[1]), values.dtype), values[:-offset]], axis=0)
        same_seq = jnp.concatenate([jnp.zeros((offset,), jnp.bool_), segment[offset:] == segment[:-offset]], axis=0)
        summed = summed + jnp.where(same_seq[:, None], shifted, 0.0) * weight[CONV - 1 - offset]
    return jax.nn.silu(summed)

def block_step(rate, state, inputs):
    x_head, b_mat, c_mat, step_size, keep_one = inputs
    state = state * keep_one
    cum = jnp.cumsum(step_size * rate[None, :], axis=0)
    scores = jnp.dot(c_mat, b_mat.T, precision=highest)
    cum_t = cum.T
    lower = jnp.arange(BLOCK)[:, None] >= jnp.arange(BLOCK)[None, :]
    diff = cum_t[:, :, None] - cum_t[:, None, :]
    decay = jnp.where(lower[None], jnp.exp(jnp.where(lower[None], diff, 0.0)), 0.0)
    weights = scores[None] * decay * step_size.T[:, None, :]
    inner = jnp.einsum('hts,shp->thp', weights, x_head, precision=highest)
    across = jnp.einsum('tn,hpn->thp', c_mat, state, precision=highest) * jnp.exp(cum)[:, :, None]
    tail = jnp.exp(cum[-1][None, :] - cum) * step_size
    fresh = jnp.einsum('shp,sn,sh->hpn', x_head, b_mat, tail, precision=highest)
    state = jnp.exp(cum[-1])[:, None, None] * state + fresh
    return (state, inner + across)

def scan_heads(x_conv, b_mat, c_mat, step_size, rate, skip, keep):
    total = x_conv.shape[0]
    heads = skip.shape[0]
    count = total // BLOCK
    x_head = x_conv.reshape(count, BLOCK, heads, HEAD)
    inputs = (x_head, b_mat.reshape(count, BLOCK, NS), c_mat.reshape(count, BLOCK, NS), step_size.reshape(count, BLOCK, heads), keep)
    start = jnp.zeros((heads, HEAD, NS), jnp.float32)
    _, y_blocks = lax.scan(jax.checkpoint(partial(block_step, rate)), start, inputs)
    y_blocks = y_blocks + x_head * skip[None, None, :, None]
    return y_blocks.reshape(total, heads * HEAD)

def replica(x_rows, length_row, params):
    gain_in, w_z, w_x, w_bc, w_dt, conv_x, conv_x_bias, conv_bc, conv_bc_bias, dt_bias, a_log, d_skip, gain_gate, w_out = params
    ends = jnp.cumsum(length_row)
    positions = jnp.arange(TOK_REP).astype(jnp.int32)
    segment = lax.optimization_barrier(jnp.sum((positions[:, None] >= ends[None, :]).astype(jnp.int32), axis=1))
    live = (positions < ends[-1]).astype(jnp.float32)
    first = segment[::BLOCK]
    last = segment[BLOCK - 1::BLOCK]
    keep = jnp.concatenate([jnp.zeros((1,), jnp.float32), (first[1:] == last[:-1]).astype(jnp.float32)])
    rstd = lax.rsqrt(lax.optimization_barrier(jnp.mean(x_rows * x_rows, axis=1, keepdims=True)) + epsilon)
    normed = low(x_rows * rstd * gain_in)
    z_pre = low_back(low(jnp.dot(normed, w_z, precision=highest)))
    x_pre = low_back(low(jnp.dot(normed, w_x, precision=highest)))
    dt_pre = low_back(low(jnp.dot(normed, w_dt, precision=highest)))
    bc_pre = low_back(low(jnp.dot(normed, w_bc, precision=highest)))
    x_conv = conv_silu(x_pre, conv_x, conv_x_bias, segment)
    bc_conv = low(conv_silu(bc_pre, conv_bc, conv_bc_bias, segment))
    step_size = jax.nn.softplus(dt_pre + dt_bias)
    y_scan = scan_heads(x_conv, bc_conv[:, :NS], bc_conv[:, NS:], step_size, -jnp.exp(a_log), d_skip, keep)
    gated = y_scan * jax.nn.silu(z_pre)
    rs_gate = lax.rsqrt(lax.optimization_barrier(jnp.mean(gated * gated, axis=1, keepdims=True)) + epsilon)
    y_out = low(gated * rs_gate * gain_gate)
    mix = low_back(jnp.dot(y_out, w_out, precision=highest))
    return x_rows + live[:, None] * mix

def replica_apply(params, items):
    return jax.checkpoint(replica)(items[0], items[1], params)

def reference(block_input, d_out, lengths, gain_in, w_z, w_x, w_bc, w_dt, conv_x, conv_x_bias, conv_bc, conv_bc_bias, dt_bias, a_log, d_skip, gain_gate, w_out):
    params = tuple((value.astype(jnp.float32) for value in (gain_in, w_z, w_x, w_bc, w_dt, conv_x, conv_x_bias, conv_bc, conv_bc_bias, dt_bias, a_log, d_skip, gain_gate, w_out)))
    x_all = block_input.astype(jnp.float32).reshape(N_DP, TOK_REP, D)

    def forward(x_rows, weights):
        return lax.map(partial(replica_apply, weights), (x_rows, lengths))
    out_all, pull = jax.vjp(forward, x_all, params)
    d_rows, grads = pull(d_out.astype(jnp.float32).reshape(N_DP, TOK_REP, D))
    return (out_all.reshape(TOKENS, D).astype(jnp.bfloat16), d_rows.reshape(TOKENS, D), grads[0], grads[1], grads[2], grads[3], grads[4], grads[5], grads[6], grads[7], grads[8], grads[9], grads[10], grads[11], grads[12], grads[13])
```

```python
from functools import partial

import jax
import jax.numpy as jnp
from jax import lax
from jax.experimental import pallas as pl
from jax.experimental.pallas import tpu as pltpu
from jax.sharding import PartitionSpec as P

HEAD = 64
NS = 128
CONV = 4
BLOCK = 256
LONGEST = 2048
HALO = 16
LANES = 128
EPS = 1e-05
F32 = jnp.float32
BF16 = jnp.bfloat16
HIGHEST = lax.Precision.HIGHEST
RC = ("row", "col")
NT = (((1,), (1,)), ((), ()))
TN = (((0,), (0,)), ((), ()))
VMEM_LIMIT = 56 * 1024 * 1024
BIAS, GAIN, SKIP, TABLE = 4, 5, 6, 8


def dot(a, b, dims=(((1,), (0,)), ((), ()))):
    return lax.dot_general(a, b, dims, preferred_element_type=F32)


def split3(v, lane, heads):
    hi = v.astype(BF16)
    left = v - hi.astype(F32)
    mid = left.astype(BF16)
    lo = (left - mid.astype(F32)).astype(BF16)
    hi, mid, lo = (p.astype(F32) for p in (hi, mid, lo))
    return jnp.where(lane < heads, hi, jnp.where(lane < 2 * heads, mid, lo)).astype(BF16)


def spread(first, width, heads):
    lane = lax.broadcasted_iota(jnp.int32, (LANES, width), 0)
    head = first + lax.broadcasted_iota(jnp.int32, (LANES, width), 1) // HEAD
    hit = (lane == head) | (lane == head + heads) | (lane == head + 2 * heads)
    return jnp.where(hit, 1.0, 0.0).astype(BF16)


def gather_heads(first, width):
    head = first + lax.broadcasted_iota(jnp.int32, (width, LANES), 0) // HEAD
    lane = lax.broadcasted_iota(jnp.int32, (width, LANES), 1)
    return jnp.where(head == lane, 1.0, 0.0).astype(BF16)


def head_sum(v, to_lanes):
    return dot(v.astype(BF16), to_lanes)


def shifted(ext, block, keep):
    start = HALO - 8 + block * BLOCK
    slab = ext[start : start + BLOCK + 8]
    row = lax.broadcasted_iota(jnp.int32, slab.shape, 0)
    slab = jnp.where(row < 8, slab * keep, slab)
    return [slab[8:]] + [pltpu.roll(slab, o, 0)[8:] for o in range(1, CONV)]


def conv_rows(parts, taps, bias):
    total = parts[0] * taps[CONV - 1 : CONV] + bias
    for o in range(1, CONV):
        total = total + parts[o] * taps[CONV - 1 - o : CONV - o]
    return total


def sigmoid(v):
    return 1.0 / (1.0 + jnp.exp(-v))


def conv_back(d_sum, taps):
    zero = jnp.zeros((8, d_sum.shape[1]), F32)
    slab = jnp.concatenate([zero, d_sum, zero], axis=0)
    rows = slab.shape[0]
    total = slab * taps[CONV - 1 : CONV]
    for o in range(1, CONV):
        total = total + pltpu.roll(slab, rows - o, 0) * taps[CONV - 1 - o : CONV - o]
    return total[: BLOCK + 8]


def prep_kernel(
    blocks, heads,
    flags, nx, wbd, taps, bias, dt_bias, rate,
    bc_pre_o, b_o, c_o, bt_o, ct_o, raw_o, dt_o, dtp_o, cum_o, cump_o, cumt_o,
):
    pre = dot(nx[...], wbd[...], NT).astype(BF16)
    bc_pre_o[...] = pre[:, : 2 * NS]
    ext = pre[:, : 2 * NS].astype(F32)
    raw = pre[HALO:, 2 * NS :].astype(F32) + dt_bias[...]
    raw_o[...] = raw
    step = jnp.maximum(raw, 0.0) + jnp.log1p(jnp.exp(-jnp.abs(raw)))
    lane = lax.broadcasted_iota(jnp.int32, step.shape, 1)
    dt_o[...] = step
    dtp_o[...] = split3(jnp.where(lane < 3 * heads, step, 0.0), lane, heads)
    scaled = step * rate[...]
    tri = jnp.where(
        lax.broadcasted_iota(jnp.int32, (BLOCK, BLOCK), 0)
        >= lax.broadcasted_iota(jnp.int32, (BLOCK, BLOCK), 1),
        1.0,
        0.0,
    )
    for b in range(blocks):
        at = slice(b * BLOCK, (b + 1) * BLOCK)
        cum = jnp.dot(tri, scaled[at], precision=HIGHEST, preferred_element_type=F32)
        cum_o[at, :] = cum
        cump_o[at, :] = split3(cum, lane[at], heads)
        cumt_o[:, at] = cum.T
        conv = conv_rows(shifted(ext, b, flags[b]), taps[...], bias[...])
        bc = (conv * sigmoid(conv)).astype(BF16)
        b_o[at, :] = bc[:, :NS]
        c_o[at, :] = bc[:, NS:]
        bc32 = bc.astype(F32)
        bt_o[:, at] = bc32[:, :NS].T.astype(BF16)
        ct_o[:, at] = bc32[:, NS:].T.astype(BF16)


def state_kernel(
    blocks, heads,
    flags, nx, w, w_other, table, dtp, cump, bt,
    pre_o, x_o, hloc_o, sent_o, fade_o,
):
    g = pl.program_id(0)
    width = x_o.shape[1]
    own = g % 2 == flags[2 * blocks].astype(jnp.int32)
    pre = dot(nx[...], jnp.where(own, w[0], w_other[0])).astype(BF16)
    pre_o[...] = pre
    ext = pre.astype(F32)
    to_cols = spread(g * (width // HEAD), width, heads)
    dt = dot(dtp[...], to_cols)
    cum = dot(cump[...], to_cols)
    carried = jnp.zeros((NS, width), F32)
    through = jnp.ones((1, width), F32)
    for b in range(blocks):
        at = slice(b * BLOCK, (b + 1) * BLOCK)
        conv = conv_rows(shifted(ext, b, flags[b]), table[:CONV], table[BIAS : BIAS + 1])
        x = conv * sigmoid(conv)
        x_o[at, :] = x.astype(BF16)
        cum_b = cum[at]
        last = cum_b[BLOCK - 1 : BLOCK]
        tail = (x * dt[at] * jnp.exp(last - cum_b)).astype(BF16)
        fade = jnp.exp(last)
        carried = carried * flags[b]
        through = through * flags[b]
        hloc_o[b] = carried.astype(BF16)
        fade_o[b : b + 1, :] = through
        fade_o[blocks + b : blocks + b + 1, :] = fade
        carried = fade * carried + dot(bt[:, at], tail)
        through = through * fade
    sent_o[:NS, :] = carried.astype(BF16)
    sent_o[NS:, :] = jnp.broadcast_to(through, (sent_o.shape[0] - NS, width)).astype(BF16)


def head_column(cum, head):
    lane = lax.broadcasted_iota(jnp.int32, cum.shape, 1)
    return jnp.sum(jnp.where(lane == head, cum, 0.0), axis=1, keepdims=True)


def stacked(v, count):
    head = lax.broadcasted_iota(jnp.int32, v.shape, 1) // HEAD
    return jnp.concatenate(
        [jnp.where(head == i, v, 0.0).astype(BF16) for i in range(count)], axis=0
    )


def inner_kernel(blocks, heads, table, b_in, c_in, x_in, dtp, cum_in, cumt_in, y_o, scores):
    g = pl.program_id(0)
    width = y_o.shape[1]
    count = width // HEAD

    @pl.when(g == 0)
    def _():
        for b in range(blocks):
            at = slice(b * BLOCK, (b + 1) * BLOCK)
            scores[b] = dot(c_in[at, :], b_in[at, :], NT)

    dt = dot(dtp[...], spread(g * count, width, heads))
    lower = lax.broadcasted_iota(jnp.int32, (BLOCK, BLOCK), 0) >= lax.broadcasted_iota(
        jnp.int32, (BLOCK, BLOCK), 1
    )
    for b in range(blocks):
        at = slice(b * BLOCK, (b + 1) * BLOCK)
        x = x_in[at, :].astype(F32)
        u = stacked(x * dt[at], count)
        cum = cum_in[at, :]
        weights = []
        for i in range(count):
            h = g * count + i
            diff = head_column(cum, h) - cumt_in[pl.ds(h, 1), at]
            decay = jnp.exp(jnp.where(lower, diff, -1e30))
            weights.append((scores[b] * decay).astype(BF16))
        y = dot(jnp.concatenate(weights, axis=1), u)
        y_o[at, :] = (y + x * table[SKIP : SKIP + 1]).astype(BF16)


def project_kernel(nx, d_mix, w, z_o, back_o):
    width = z_o.shape[1]
    z_o[...] = dot(nx[HALO:, :], w[0, :width], NT).astype(BF16)
    back_o[...] = dot(d_mix[...], w[0, width:], NT).astype(BF16)


def middle_kernel(
    heads,
    table, y_in, z_in, x_in, back_in, c_in, ct_in, cump, hloc, before, fade,
    yout_o, dy_o, dz_o, row_o, dc_o, dst_o, sums_o, sent_o,
):
    b = pl.program_id(0)
    width = y_in.shape[1]
    through = fade[pl.ds(b, 1), :]
    enter = (through * before[:NS].astype(F32) + hloc[0].astype(F32)).astype(BF16)
    grow = jnp.exp(dot(cump[...], spread(0, width, heads)))
    across = dot(c_in[...], enter) * grow
    y = y_in[...].astype(F32) + across
    z = z_in[...].astype(F32)
    gate = sigmoid(z)
    silu = z * gate
    gated = y * silu
    rs = lax.rsqrt(jnp.sum(gated * gated, axis=1, keepdims=True) / width + EPS)
    unit = gated * rs
    gain = table[GAIN : GAIN + 1]
    yout_o[...] = (unit * gain).astype(BF16)
    back = back_in[...].astype(F32)
    d_unit = back * gain
    along = jnp.sum(d_unit * gated, axis=1, keepdims=True) / width
    d_gated = rs * d_unit - gated * (rs * rs * rs * along)
    dy = d_gated * silu
    dy_o[...] = dy.astype(BF16)
    dz_o[...] = (d_gated * y * (gate * (1.0 + z * (1.0 - gate)))).astype(BF16)
    row_o[...] = head_sum(dy * across, gather_heads(0, width))
    grown = (dy * grow).astype(BF16)
    dc_o[...] = dot(grown, enter, NT)
    dst = dot(ct_in[...], grown)
    dst_o[0] = dst.astype(BF16)

    @pl.when(b == 0)
    def _():
        sums_o[...] = jnp.zeros_like(sums_o)
        sent_o[...] = jnp.zeros_like(sent_o)

    sums_o[0:1] += jnp.sum(back * unit, axis=0, keepdims=True)
    sums_o[1:2] += jnp.sum(dy * x_in[...].astype(F32), axis=0, keepdims=True)
    sent_o[...] += through * dst


def weights_kernel(blocks, flags, nx, d_mix, dz, yout, keep_o, give_o):
    g = pl.program_id(0)
    width = dz.shape[1]
    own = g % 2 == flags[2 * blocks].astype(jnp.int32)
    dw_z = dot(dz[...], nx[HALO:, :], TN).astype(BF16)
    dw_out = dot(yout[...], d_mix[...], TN).astype(BF16)

    @pl.when(own)
    def _():
        keep_o[0, :width] = dw_z
        keep_o[0, width:] = dw_out

    @pl.when(jnp.logical_not(own))
    def _():
        give_o[0, :width] = dw_z
        give_o[0, width:] = dw_out


def mix_kernel(blocks, flags, w, dz, yout, x_rows, dn_o, out_o):
    inner = dz.shape[1]
    width = inner // w.shape[0]
    tile = out_o.shape[1]
    dn_o[...] = dot(dz[...], w[:, :width, :].reshape(inner, tile))
    mix = dot(yout[...], w[:, width:, :].reshape(inner, tile))
    for b in range(blocks):
        at = slice(b * BLOCK, (b + 1) * BLOCK)
        live = flags[blocks + b]
        out_o[at, :] = (x_rows[at, :].astype(F32) + live * mix[at]).astype(BF16)


def norm_back_kernel(blocks, flags, w, w_other, d_pre_a, d_pre_b, dn_z, dn_o):
    first = flags[2 * blocks] == 0.0
    members = []
    for z in range(w.shape[0]):
        members += [jnp.where(first, w[z], w_other[z]), jnp.where(first, w_other[z], w[z])]
    half = len(members) // 2
    total = dot(d_pre_a[...], jnp.concatenate(members[:half], axis=1), NT)
    total += dot(d_pre_b[...], jnp.concatenate(members[half:], axis=1), NT)
    dn_o[:HALO, :] = total[:HALO]
    dn_o[HALO:, :] = total[HALO:] + dn_z[...]


def inner_back_kernel(
    blocks, heads,
    b_in, c_in, x_in, dy_in, dtp, cum_in, cumt_in,
    du_o, dbc_o, rows_o, cols_o, scores, d_scores,
):
    g = pl.program_id(0)
    width = du_o.shape[1]
    count = width // HEAD

    @pl.when(g == 0)
    def _():
        d_scores[...] = jnp.zeros_like(d_scores)
        cols_o[...] = jnp.zeros_like(cols_o)
        for b in range(blocks):
            at = slice(b * BLOCK, (b + 1) * BLOCK)
            scores[b] = dot(b_in[at, :], c_in[at, :], NT)

    rows_o[...] = jnp.zeros_like(rows_o)
    dt = dot(dtp[...], spread(g * count, width, heads))
    lower = lax.broadcasted_iota(jnp.int32, (BLOCK, BLOCK), 0) <= lax.broadcasted_iota(
        jnp.int32, (BLOCK, BLOCK), 1
    )
    for b in range(blocks):
        at = slice(b * BLOCK, (b + 1) * BLOCK)
        u = (x_in[at, :].astype(F32) * dt[at]).astype(BF16)
        dy = stacked(dy_in[at, :].astype(F32), count)
        d_w = dot(u, dy, NT)
        cum = cum_in[at, :]
        lane = lax.broadcasted_iota(jnp.int32, cum.shape, 1)
        cols = cols_o[at, :]
        weights = []
        for i in range(count):
            h = g * count + i
            diff = cumt_in[pl.ds(h, 1), at] - head_column(cum, h)
            decay = jnp.exp(jnp.where(lower, diff, -1e30))
            weights.append((scores[b] * decay).astype(BF16))
            d_score = d_w[:, i * BLOCK : (i + 1) * BLOCK] * decay
            d_scores[b] += d_score
            both = d_score * scores[b]
            rows_o[0, i : i + 1, at] = jnp.sum(both, axis=0, keepdims=True)
            cols = jnp.where(lane == h, jnp.sum(both, axis=1, keepdims=True), cols)
        cols_o[at, :] = cols
        du_o[at, :] = dot(jnp.concatenate(weights, axis=1), dy).astype(BF16)

    @pl.when(g == pl.num_programs(0) - 1)
    def _():
        for b in range(blocks):
            at = slice(b * BLOCK, (b + 1) * BLOCK)
            ds = d_scores[b].astype(BF16)
            dbc_o[at, :NS] = dot(ds, c_in[at, :])
            dbc_o[at, NS:] = dot(ds, b_in[at, :], TN)


def back_kernel(
    blocks, heads, base,
    flags, db_in, q_in, gdt_in, nx_t, table, pre_in, dy_in, du_in, b_in, dtp, cump, hloc, before, after, dst, fade,
    keep_o, give_o, d_pre_o, db_o, q_o, gdt_o, fdh_o, dtap_o, d_ext,
):
    g = pl.program_id(0)
    width = dy_in.shape[1]
    first = (base + g) * (width // HEAD)

    @pl.when(g == 0)
    def _():
        db_o[...] = db_in[...]
        q_o[...] = q_in[...]
        gdt_o[...] = gdt_in[...]

    to_cols = spread(first, width, heads)
    to_lanes = gather_heads(first, width)
    dt_all = dot(dtp[...], to_cols)
    cum_all = dot(cump[...], to_cols)
    ext = pre_in[...].astype(F32)
    taps = table[:CONV]
    skip = table[SKIP : SKIP + 1]
    d_states = [None] * blocks
    d_state = after[:NS].astype(F32)
    for b in reversed(range(blocks)):
        d_states[b] = d_state
        fade_b = fade[blocks + b : blocks + b + 1]
        d_state = flags[b] * (fade_b * d_state + dst[b].astype(F32))
    d_ext[:HALO, :] = jnp.zeros((HALO, width), F32)
    d_taps = [jnp.zeros((1, width), F32) for _ in range(CONV + 1)]
    fdh_o[...] = jnp.zeros_like(fdh_o)
    for b in range(blocks):
        at = slice(b * BLOCK, (b + 1) * BLOCK)
        enter = fade[b : b + 1] * before[:NS].astype(F32) + hloc[b].astype(F32)
        fdh_o[b : b + 1, :] = fade[blocks + b : blocks + b + 1] * jnp.sum(
            enter * d_states[b], axis=0, keepdims=True
        )
        d_st = d_states[b].astype(BF16)
        parts = shifted(ext, b, flags[b])
        conv = conv_rows(parts, taps, table[BIAS : BIAS + 1])
        sig = sigmoid(conv)
        x = conv * sig
        dt = dt_all[at]
        cum = cum_all[at]
        tail = jnp.exp(cum[BLOCK - 1 : BLOCK] - cum)
        u = x * dt
        du_state = dot(b_in[at, :], d_st) * tail
        du = du_in[at, :].astype(F32) + du_state
        db_o[at, :] += dot((u * tail).astype(BF16), d_st, NT)
        q_o[at, :] += head_sum(u * du_state, to_lanes)
        gdt_o[at, :] += head_sum(x * du, to_lanes)
        dx = dt * du + skip * dy_in[at, :].astype(F32)
        d_sum = dx * (sig * (1.0 + conv * (1.0 - sig)))
        for o in range(CONV):
            d_taps[CONV - 1 - o] += jnp.sum(d_sum * parts[o], axis=0, keepdims=True)
        d_taps[CONV] += jnp.sum(d_sum, axis=0, keepdims=True)
        carried = conv_back(d_sum, taps)
        start = HALO + b * BLOCK
        d_ext[start - 8 : start, :] += flags[b] * carried[:8]
        d_ext[start : start + BLOCK, :] = carried[8:]
    dtap_o[...] = jnp.concatenate(d_taps + [jnp.zeros((3, width), F32)], axis=0)
    d_pre = d_ext[...].astype(BF16)
    d_pre_o[...] = d_pre
    dw = dot(nx_t[...], d_pre).astype(BF16)
    own = g % 2 == flags[2 * blocks].astype(jnp.int32)

    @pl.when(own)
    def _():
        keep_o[0] = dw

    @pl.when(jnp.logical_not(own))
    def _():
        give_o[0] = dw


def last_kernel(
    blocks, heads,
    flags, nx, wbd, taps_in, bias, rate, bc_pre, dbc, dc, db, raw, step_in,
    rows, cols, row, q, gdt, fdh, dn_x, x_ext, rstd,
    dw_o, dn_o, gain_o, dtap_o, ddt_o, d_ext,
):
    taps = taps_in[...]
    ext = bc_pre[...].astype(F32)
    width = ext.shape[1]
    d_ext[:HALO, :] = jnp.zeros((HALO, d_ext.shape[1]), F32)
    d_taps = [jnp.zeros((1, width), F32) for _ in range(CONV + 1)]
    bias_sum = jnp.zeros((1, LANES), F32)
    rate_sum = jnp.zeros((1, LANES), F32)
    row_i = lax.broadcasted_iota(jnp.int32, (BLOCK, BLOCK), 0)
    col_i = lax.broadcasted_iota(jnp.int32, (BLOCK, BLOCK), 1)
    onward = jnp.where(row_i <= col_i, 1.0, 0.0)
    earlier = jnp.where(row_i > col_i, 1.0, 0.0)
    lane = lax.broadcasted_iota(jnp.int32, (BLOCK, LANES), 1)
    faded = jnp.dot(
        fdh[...], gather_heads(0, fdh.shape[1]).astype(F32), precision=HIGHEST,
        preferred_element_type=F32,
    )
    for b in range(blocks):
        at = slice(b * BLOCK, (b + 1) * BLOCK)
        start = HALO + b * BLOCK
        flow = rows[at, :] - cols[at, :] + row[at, :]
        d_a = (
            jnp.dot(onward, flow, precision=HIGHEST, preferred_element_type=F32)
            + jnp.dot(earlier, q[at, :], precision=HIGHEST, preferred_element_type=F32)
            + faded[b : b + 1]
        )
        step = step_in[at, :]
        d_step = gdt[at, :] + rate[...] * d_a
        d_raw = jnp.where(lane < heads, d_step * sigmoid(raw[at, :]), 0.0)
        bias_sum += jnp.sum(d_raw, axis=0, keepdims=True)
        rate_sum += jnp.sum(step * d_a, axis=0, keepdims=True)
        d_ext[start : start + BLOCK, 2 * NS :] = d_raw
        parts = shifted(ext, b, flags[b])
        conv = conv_rows(parts, taps, bias[...])
        sig = sigmoid(conv)
        d_bc = dbc[at, :] + jnp.concatenate([db[at, :], dc[at, :]], axis=1)
        d_sum = d_bc * (sig * (1.0 + conv * (1.0 - sig)))
        for o in range(CONV):
            d_taps[CONV - 1 - o] += jnp.sum(d_sum * parts[o], axis=0, keepdims=True)
        d_taps[CONV] += jnp.sum(d_sum, axis=0, keepdims=True)
        carried = conv_back(d_sum, taps)
        d_ext[start - 8 : start, : 2 * NS] += flags[b] * carried[:8]
        d_ext[start : start + BLOCK, : 2 * NS] = carried[8:]
    dtap_o[...] = jnp.concatenate(d_taps + [jnp.zeros((3, width), F32)], axis=0)
    ddt_o[...] = jnp.concatenate(
        [bias_sum, rate_sum * rate[...], jnp.zeros((6, LANES), F32)], axis=0
    )
    d_pre = d_ext[...].astype(BF16)
    dw_o[...] = dot(d_pre, nx[...], TN).astype(BF16)
    total = dn_x[...] + dot(d_pre, wbd[...])
    dn_o[...] = total
    gain_o[...] = jnp.sum(total * (x_ext[...].astype(F32) * rstd[...]), axis=0, keepdims=True)


def whole(shape):
    rank = len(shape)
    return pl.BlockSpec(shape, lambda *_: (0,) * rank)


SMEM = pl.BlockSpec(memory_space=pltpu.SMEM)


def cols_of(rows, width):
    return pl.BlockSpec((rows, width), lambda g: (0, g))


def member_of(rows, width):
    return pl.BlockSpec((1, rows, width), lambda g: (g, 0, 0))


def pair_of(rows, width):
    return pl.BlockSpec((1, rows, width), lambda g: (g // 2, 0, 0))


def call(kernel, grid, ins, outs, scratch, name, us, *args, after=()):
    count = len(args)

    def body(*refs):
        kernel(*refs[:count], *refs[count + len(after) :])

    return pl.pallas_call(
        body,
        grid=grid,
        in_specs=list(ins) + [pl.BlockSpec(memory_space=pl.ANY)] * len(after),
        out_specs=[spec for _, _, spec in outs],
        out_shape=[jax.ShapeDtypeStruct(shape, dtype) for shape, dtype, _ in outs],
        scratch_shapes=scratch,
        compiler_params=pltpu.CompilerParams(vmem_limit_bytes=VMEM_LIMIT),
        cost_estimate=pl.CostEstimate(
            flops=int(us * 1.1e9), bytes_accessed=int(us * 1e6), transcendentals=0
        ),
        name=name,
    )(*args, *after)


def state_scan(own, members, tokens, forward, beside=()):
    def moved(v, by):
        pairs = [(i, i + by) for i in range(members - by)]
        if not forward:
            pairs = [(b, a) for a, b in pairs]
        return lax.ppermute(v, RC, pairs)

    reach = min(members - 1, -(-LONGEST // tokens))
    is_term = lax.broadcasted_iota(jnp.int32, own.shape, 0) < NS
    steps = []
    span = 1
    while span < reach:
        got = moved(own, span).astype(F32)
        if len(steps) < len(beside):
            own, _ = lax.optimization_barrier((own, beside[len(steps)]))
        held = own.astype(F32)
        own = (jnp.where(is_term, held, 0.0) + held[NS : NS + 1] * got).astype(BF16)
        steps.append(own)
        span *= 2
    steps.append(moved(own, 1))
    return steps


def thrice(v):
    hi = lax.optimization_barrier(v.astype(BF16))
    left = v - hi.astype(F32)
    mid = lax.optimization_barrier(left.astype(BF16))
    lo = (left - mid.astype(F32)).astype(BF16)
    return jnp.stack([hi, mid, lo])


def halves(v, axis):
    half = v.shape[axis] // 2
    return lax.slice_in_dim(v, 0, half, axis=axis), lax.slice_in_dim(v, half, None, axis=axis)


def dp_bits():
    return [1 << i for i in range((lax.axis_size("dp") - 1).bit_length())]


def across_dp(v, bit):
    return lax.ppermute(v, "dp", [(i, i ^ bit) for i in range(lax.axis_size("dp"))])


def set_bit(bit):
    return (lax.axis_index("dp") // bit) % 2 == 1


def double(v, bit, axis):
    got = across_dp(v, bit)
    up = set_bit(bit)
    return jnp.concatenate([jnp.where(up, got, v), jnp.where(up, v, got)], axis=axis)


def doubled(v, bits, axis):
    for bit in bits:
        v = double(v, bit, axis)
    return v


def to_halve(v, bit, axis):
    low, high = halves(v, axis)
    up = set_bit(bit)
    return jnp.where(up, high, low), jnp.where(up, low, high)


def summed(stays, goes, bit):
    return (stays.astype(F32) + across_dp(goes, bit).astype(F32)).astype(BF16)


def along_row(v, by):
    rows = lax.axis_size("row")
    return lax.ppermute(v, "row", [(i, (i + by) % rows) for i in range(rows)])


def other_col(v):
    return lax.ppermute(v, "col", [(0, 1), (1, 0)])


def gather_rows(v):
    rows = lax.axis_size("row")
    row = lax.axis_index("row")
    out = jnp.zeros((rows,) + v.shape, v.dtype)
    for by in range(rows):
        piece = v if by == 0 else along_row(v, by)
        out = lax.dynamic_update_index_in_dim(out, piece, (row - by) % rows, 0)
    return out


def row_pieces(v):
    rows = lax.axis_size("row")
    row = lax.axis_index("row")
    return tuple(
        lax.dynamic_index_in_dim(v, (row + by) % rows, 0, keepdims=False) for by in range(rows)
    )


def sum_rows(pieces):
    terms = [(p if by == 0 else along_row(p, by)).astype(F32) for by, p in enumerate(pieces)]
    while len(terms) > 1:
        half = len(terms) // 2
        terms = [terms[i] + terms[i + half] for i in range(half)]
    return terms[0]


def reduce_shards(parts):
    bits = dp_bits()
    sums = [(k.astype(F32) + other_col(v).astype(F32)).astype(BF16) for k, v in parts]
    now = halves(jnp.concatenate(sums, axis=0), 1)
    for one, two in zip(bits[::-1], bits):
        a, b, c, d = yield to_halve(now[0], one, 1) + to_halve(now[1], two, 1)
        now = summed(a, b, one), summed(c, d, two)
    cut = now[0].shape[1]
    pieces = yield row_pieces(jnp.concatenate(now, axis=1))
    part = sum_rows(pieces).astype(BF16)
    now = yield part[:cut], part[cut:]
    for one, two in zip(bits, bits[::-1]):
        now = yield double(now[0], one, 0), double(now[1], two, 0)


def reduce_small(v):
    even, odd = v[:, 0], v[:, 1]
    first = lax.axis_index("col") == 0
    both = jnp.where(first, even, odd).astype(F32) + other_col(
        jnp.where(first, odd, even)
    ).astype(F32)
    pieces = yield row_pieces(both.astype(BF16))
    now = yield (sum_rows(pieces),)
    for bit in dp_bits():
        now = yield (now[0] + across_dp(now[0], bit),)


def in_step(runs, states):
    running = list(range(len(runs)))
    while running:
        left = []
        for i in running:
            try:
                states[i] = next(runs[i]) if states[i] is None else runs[i].send(states[i])
                left.append(i)
            except StopIteration:
                pass
        running = left
        if running:
            tied = lax.optimization_barrier([states[i] for i in running])
            for i, value in zip(running, tied):
                states[i] = value
    return states


def gather_shards(v):
    bits = dp_bits()
    me = lax.axis_index("dp")
    turned = sum(((me // bit) % 2) * back for bit, back in zip(bits, bits[::-1]))
    first, second = halves(v, 0)
    rows = first.shape[0] // lax.axis_size("dp")
    mine = jnp.concatenate(
        [lax.dynamic_slice_in_dim(first, me * rows, rows, 0),
         lax.dynamic_slice_in_dim(second, turned * rows, rows, 0)], axis=0
    )
    got = gather_rows(mine)
    first = doubled(got[:, :rows], bits, 1)
    second = doubled(got[:, rows:], bits[::-1], 1)
    own = jnp.concatenate([first, second], axis=1)
    return own, other_col(own)


def on_device(
    block_input, d_out, lengths, gain_in, w_z, w_x, w_bc, w_dt, conv_x, conv_x_bias,
    conv_bc, conv_bc_bias, dt_bias, a_log, d_skip, gain_gate, w_out,
):
    members = lax.axis_size(RC)
    place = lax.axis_index(RC)
    tokens, model = block_input.shape
    blocks = tokens // BLOCK
    width = w_x.shape[1]
    inner = width * members
    group_heads = w_dt.shape[1]
    heads = group_heads * members
    bc_cols = w_bc.shape[1]
    ext_rows = tokens + HALO

    small = jnp.concatenate(
        [conv_x.reshape(-1), conv_x_bias, gain_gate, conv_bc.reshape(-1), conv_bc_bias,
         dt_bias, a_log, d_skip]
    )
    small_rows = -(-small.shape[0] // model)
    parts = thrice(jnp.pad(small, (0, small_rows * model - small.shape[0])))
    side = bc_cols + group_heads
    rows1 = side + 3 * small_rows
    pack1 = jnp.concatenate(
        [w_bc.T, w_dt.T, parts.reshape(3 * small_rows, model),
         jnp.zeros((-rows1 % 16, model), BF16)], axis=0
    )
    col = lax.axis_index("col")
    own1 = gather_rows(pack1)
    other1 = other_col(own1)
    all1 = jnp.where(
        col == 0, jnp.stack([own1, other1], axis=1), jnp.stack([other1, own1], axis=1)
    ).reshape(members, -1, model)
    wx_own, wx_other = gather_shards(w_x)
    pack2 = jnp.concatenate([w_z.T, w_out], axis=0)
    all2 = lax.all_gather(pack2, RC, axis=0)

    ends = jnp.cumsum(lengths[0])
    firsts = jnp.arange(members * blocks, dtype=jnp.int32) * BLOCK

    def segment(at):
        return jnp.sum((at[:, None] >= ends[None, :]).astype(jnp.int32), axis=1)

    kept = (segment(firsts) == segment(firsts - 1)) & (firsts > 0)
    both = jnp.stack([kept, firsts < ends[-1]]).astype(F32)
    flags = lax.dynamic_slice(both, (0, place * blocks), (2, blocks)).reshape(-1)
    flags = jnp.concatenate([flags, col.astype(F32)[None]])

    ahead = [(i, i + 1) for i in range(members - 1)]
    back = [(i + 1, i) for i in range(members - 1)]
    tail_rows = lax.ppermute(block_input[tokens - HALO :], RC, ahead)
    x_ext = jnp.concatenate([tail_rows, block_input], axis=0)
    x32 = x_ext.astype(F32)
    rstd = lax.rsqrt(jnp.mean(x32 * x32, axis=1, keepdims=True) + EPS)
    nx = (x32 * rstd * gain_in).astype(BF16)
    nx_t = nx.T
    live = jnp.repeat(flags[blocks : 2 * blocks], BLOCK)[:, None]
    d_mix = (d_out.astype(F32) * live).astype(BF16)

    w_bc_t = all1[:, :bc_cols].reshape(-1, model)
    w_dt_t = all1[:, bc_cols:side].reshape(-1, model)
    wbd = jnp.concatenate(
        [w_bc_t, w_dt_t, w_dt_t, w_dt_t, jnp.zeros((LANES - 3 * heads, model), BF16)], axis=0
    )
    pieces = all1[:, side : side + 3 * small_rows].astype(F32)
    pieces = pieces.reshape(members, 3, small_rows * model)
    small_all = pieces[:, 0] + pieces[:, 1] + pieces[:, 2]
    sizes = [conv_x.size, width, width, conv_bc.size, bc_cols, group_heads, group_heads, group_heads]
    cuts = [sum(sizes[:i]) for i in range(len(sizes) + 1)]
    s_conv, s_bias, s_gain, s_cbc, s_cbias, s_dtb, s_alog, s_skip = (
        small_all[:, cuts[i] : cuts[i + 1]] for i in range(len(sizes))
    )
    skip_cols = jnp.repeat(s_skip.reshape(-1), HEAD)[None]
    table = jnp.concatenate(
        [s_conv.reshape(members, CONV, width).transpose(1, 0, 2).reshape(CONV, inner),
         s_bias.reshape(1, inner), s_gain.reshape(1, inner), skip_cols,
         jnp.zeros((1, inner), F32)], axis=0
    )
    taps_bc = s_cbc.reshape(members, CONV, bc_cols).transpose(1, 0, 2).reshape(CONV, 2 * NS)
    bias_bc = s_cbias.reshape(1, 2 * NS)

    def lanes(v):
        return jnp.pad(jnp.tile(v.reshape(1, heads), (1, 3)), ((0, 0), (0, LANES - 3 * heads)))

    dtb = lanes(s_dtb)
    rate = lanes(-jnp.exp(s_alog))

    (bc_pre, b16, c16, bt, ct, raw, step, dtp, cum, cump, cumt) = call(
        partial(prep_kernel, blocks, heads), (1,),
        [SMEM, whole((ext_rows, model)), whole(wbd.shape), whole(taps_bc.shape),
         whole(bias_bc.shape), whole((1, LANES)), whole((1, LANES))],
        [((ext_rows, 2 * NS), BF16, whole((ext_rows, 2 * NS))),
         ((tokens, NS), BF16, whole((tokens, NS))),
         ((tokens, NS), BF16, whole((tokens, NS))),
         ((NS, tokens), BF16, whole((NS, tokens))),
         ((NS, tokens), BF16, whole((NS, tokens))),
         ((tokens, LANES), F32, whole((tokens, LANES))),
         ((tokens, LANES), F32, whole((tokens, LANES))),
         ((tokens, LANES), BF16, whole((tokens, LANES))),
         ((tokens, LANES), F32, whole((tokens, LANES))),
         ((tokens, LANES), BF16, whole((tokens, LANES))),
         ((LANES, tokens), F32, whole((LANES, tokens)))],
        [], "prep", 4, flags, nx, wbd, taps_bc, bias_bc, dtb, rate,
    )
    lane_rows = whole((tokens, LANES))
    sent_rows = NS + 16
    x_pre, x16, hloc, own, fade = call(
        partial(state_kernel, blocks, heads), (members,),
        [SMEM, whole((ext_rows, model)), pair_of(model, width), pair_of(model, width),
         cols_of(TABLE, width), lane_rows, lane_rows, whole((NS, tokens))],
        [((ext_rows, inner), BF16, cols_of(ext_rows, width)),
         ((tokens, inner), BF16, cols_of(tokens, width)),
         ((blocks, NS, inner), BF16, pl.BlockSpec((blocks, NS, width), lambda g: (0, 0, g))),
         ((sent_rows, inner), BF16, cols_of(sent_rows, width)),
         ((2 * blocks, inner), F32, cols_of(2 * blocks, width))],
        [], "states", 12, flags, nx, wx_own, wx_other, table, dtp, cump, bt,
    )
    before = state_scan(own, members, tokens, True)[-1]
    (y_loc,) = call(
        partial(inner_kernel, blocks, heads), (members,),
        [cols_of(TABLE, width), whole((tokens, NS)), whole((tokens, NS)), cols_of(tokens, width),
         lane_rows, lane_rows, whole((LANES, tokens))],
        [((tokens, inner), BF16, cols_of(tokens, width))],
        [pltpu.VMEM((blocks, BLOCK, BLOCK), F32)], "inner", 9,
        table, b16, c16, x16, dtp, cum, cumt,
    )
    z_pre, d_yout = call(
        project_kernel, (members,),
        [whole((ext_rows, model)), whole((tokens, model)), member_of(2 * width, model)],
        [((tokens, inner), BF16, cols_of(tokens, width))] * 2,
        [], "project", 11, nx, d_mix, all2,
    )

    def rows_of(cols):
        return pl.BlockSpec((BLOCK, cols), lambda b: (b, 0))

    y_out, dy, dz, row, dc, dst, sums, grad_own = call(
        partial(middle_kernel, heads), (blocks,),
        [whole((TABLE, inner)), rows_of(inner), rows_of(inner), rows_of(inner), rows_of(inner),
         rows_of(NS), pl.BlockSpec((NS, BLOCK), lambda b: (0, b)), rows_of(LANES),
         pl.BlockSpec((1, NS, inner), lambda b: (b, 0, 0)), whole((sent_rows, inner)),
         whole((2 * blocks, inner))],
        [((tokens, inner), BF16, rows_of(inner)),
         ((tokens, inner), BF16, rows_of(inner)),
         ((tokens, inner), BF16, rows_of(inner)),
         ((tokens, LANES), F32, rows_of(LANES)),
         ((tokens, NS), F32, rows_of(NS)),
         ((blocks, NS, inner), BF16, pl.BlockSpec((1, NS, inner), lambda b: (b, 0, 0))),
         ((8, inner), F32, whole((8, inner))),
         ((NS, inner), F32, whole((NS, inner)))],
        [], "middle", 14, table, y_loc, z_pre, x16, d_yout, c16, ct, cump, hloc, before, fade,
    )
    (keep2, give2) = call(
        partial(weights_kernel, blocks), (members,),
        [SMEM, whole((ext_rows, model)), whole((tokens, model)),
         cols_of(tokens, width), cols_of(tokens, width)],
        [((members // 2, 2 * width, model), BF16, pair_of(2 * width, model)),
         ((members // 2, 2 * width, model), BF16, pair_of(2 * width, model))],
        [], "weights", 10, flags, nx, d_mix, dz, y_out,
    )
    grad_own = jnp.concatenate([grad_own.astype(BF16), own[NS:]], axis=0)
    scan = state_scan(grad_own, members, tokens, False, (keep2,))
    run2 = reduce_shards([(keep2, give2)])
    tile = model // 4
    state2 = next(run2)
    du, dbc, rows, cols = call(
        partial(inner_back_kernel, blocks, heads), (members,),
        [whole((tokens, NS)), whole((tokens, NS)), cols_of(tokens, width), cols_of(tokens, width),
         lane_rows, lane_rows, whole((LANES, tokens))],
        [((tokens, inner), BF16, cols_of(tokens, width)),
         ((tokens, 2 * NS), F32, whole((tokens, 2 * NS))),
         ((members, 8, tokens), F32, member_of(8, tokens)),
         ((tokens, LANES), F32, lane_rows)],
        [pltpu.VMEM((blocks, BLOCK, BLOCK), F32), pltpu.VMEM((blocks, BLOCK, BLOCK), F32)],
        "inner_back", 12, b16, c16, x16, dy, dtp, cum, cumt, after=(scan[0], keep2),
    )
    dn_z, block_out = call(
        partial(mix_kernel, blocks), (4,),
        [SMEM, pl.BlockSpec((members, 2 * width, tile), lambda n: (0, 0, n)),
         whole((tokens, inner)), whole((tokens, inner)), cols_of(tokens, tile)],
        [((tokens, model), F32, cols_of(tokens, tile)),
         ((tokens, model), BF16, cols_of(tokens, tile))],
        [], "mix", 9, flags, all2, dz, y_out, block_input, after=(scan[-2], du) + state2,
    )
    after = scan[-1]
    rows = jnp.pad(
        rows[:, :group_heads].reshape(heads, tokens).T, ((0, 0), (0, LANES - heads))
    )
    half = members // 2

    def run_back(base, sums_in, waits):
        def at(rows_in):
            return pl.BlockSpec((rows_in, width), lambda g: (0, base + g))

        three = pl.BlockSpec((blocks, NS, width), lambda g: (0, 0, base + g))
        wide = half * width
        return call(
            partial(back_kernel, blocks, heads, base), (half,),
            [SMEM, whole((tokens, NS)), lane_rows, lane_rows, whole((model, ext_rows)), at(TABLE),
             at(ext_rows), at(tokens), at(tokens), whole((tokens, NS)), lane_rows, lane_rows,
             three, at(sent_rows), at(sent_rows), three, at(2 * blocks)],
            [((half // 2, model, width), BF16, pair_of(model, width)),
             ((half // 2, model, width), BF16, pair_of(model, width)),
             ((ext_rows, wide), BF16, cols_of(ext_rows, width)),
             ((tokens, NS), F32, whole((tokens, NS))),
             ((tokens, LANES), F32, lane_rows),
             ((tokens, LANES), F32, lane_rows),
             ((8, wide), F32, cols_of(8, width)),
             ((8, wide), F32, cols_of(8, width))],
            [pltpu.VMEM((ext_rows, width), F32)], "back", 11,
            flags, *sums_in, nx_t, table, x_pre, dy, du, b16, dtp, cump, hloc, before, after, dst,
            fade, after=waits,
        )

    zero = jnp.zeros((tokens, LANES), F32)
    keep1, give1, d_xpre1, *sums1, fdh1, dtaps1 = run_back(0, (zero, zero, zero), (dn_z,))
    state2 = run2.send(state2)
    keep3, give3, d_xpre3, *sums3, fdh3, dtaps3 = run_back(half, sums1, state2)
    db, q, gdt = sums3
    fdh = jnp.concatenate([fdh1, fdh3], axis=1)
    dtaps = jnp.concatenate([dtaps1, dtaps3], axis=1)
    run1 = reduce_shards([(keep1, give1), (keep3, give3)])
    state2 = run2.send(state2)
    tall = pl.BlockSpec((members // 2, tile, width), lambda n: (0, n, 0))
    half_rows = whole((ext_rows, half * width))
    (dn_x,) = call(
        partial(norm_back_kernel, blocks), (4,),
        [SMEM, tall, tall, half_rows, half_rows, cols_of(tokens, tile)],
        [((ext_rows, model), F32, cols_of(ext_rows, tile))],
        [], "norm_back", 6, flags, wx_own, wx_other, d_xpre1, d_xpre3, dn_z, after=state2,
    )
    state1 = next(run1)
    bd = 2 * NS + LANES
    ins = [nx, wbd, taps_bc, bias_bc, rate, bc_pre, dbc, dc, db, raw, step, rows, cols, row, q,
           gdt, fdh, dn_x, x_ext, rstd]
    dw_bd, d_norm, gain_part, dtaps_bc, ddt = call(
        partial(last_kernel, blocks, heads), (1,),
        [SMEM] + [whole(v.shape) for v in ins],
        [((bd, model), BF16, whole((bd, model))),
         ((ext_rows, model), F32, whole((ext_rows, model))),
         ((1, model), F32, whole((1, model))),
         ((8, 2 * NS), F32, whole((8, 2 * NS))),
         ((8, LANES), F32, whole((8, LANES)))],
        [pltpu.VMEM((ext_rows, bd), F32)], "last", 9, flags, *ins, after=state1,
    )

    d_skip_all = sums[1].reshape(members, group_heads, HEAD).sum(axis=2)

    def by_member(v, wide):
        return v.reshape(v.shape[0], members, wide).transpose(1, 0, 2).reshape(members, -1)

    small_grads = jnp.concatenate(
        [by_member(dtaps[:CONV], width), by_member(dtaps[CONV : CONV + 1], width),
         by_member(sums[0:1], width), by_member(dtaps_bc[:CONV], bc_cols),
         by_member(dtaps_bc[CONV : CONV + 1], bc_cols),
         ddt[0, :heads].reshape(members, -1), ddt[1, :heads].reshape(members, -1), d_skip_all],
        axis=1,
    )
    small_grads = jnp.pad(
        small_grads, ((0, 0), (0, small_rows * model - small_grads.shape[1]))
    ).reshape(members, small_rows, model)
    extra = jnp.concatenate(
        [dw_bd[: 2 * NS].reshape(members, bc_cols, model),
         dw_bd[2 * NS : 2 * NS + heads].reshape(members, group_heads, model),
         small_grads.astype(BF16),
         jnp.broadcast_to(gain_part[None], (members, 1, model)).astype(BF16)], axis=1,
    )
    extra = jnp.pad(extra, ((0, 0), (0, -extra.shape[1] % 16), (0, 0)))
    run3 = reduce_small(extra.reshape(members // 2, 2, -1, model))
    states = in_step([run1, run2, run3], [state1, state2, None])
    g1, g2, g3 = (jnp.concatenate(v, axis=0).astype(F32) for v in states)

    from_next = lax.ppermute(d_norm[:HALO], RC, back)
    d_normed = d_norm[HALO:]
    d_normed = jnp.concatenate(
        [d_normed[: tokens - HALO], d_normed[tokens - HALO :] + from_next], axis=0
    )
    x_rows = block_input.astype(F32)
    r_own = rstd[HALO:]
    d_v = d_normed * gain_in
    d_x = (
        d_out.astype(F32) + r_own * d_v
        - x_rows * r_own**3 * jnp.mean(d_v * x_rows, axis=1, keepdims=True)
    )
    flat = g3[side : side + small_rows].reshape(-1)
    s = [flat[cuts[i] : cuts[i + 1]] for i in range(len(sizes))]
    return (
        block_out,
        d_x,
        g3[side + small_rows],
        g2[:width].T,
        g1,
        g3[:bc_cols].T,
        g3[bc_cols:side].T,
        s[0].reshape(CONV, width),
        s[1],
        s[3].reshape(CONV, bc_cols),
        s[4],
        s[5],
        s[6],
        s[7],
        s[2],
        g2[width:],
    )


def solution(mesh):
    placed = (
        P(("dp", "row", "col"), None),
        P(("dp", "row", "col"), None),
        P("dp", None),
        P(),
        P(None, ("row", "col")),
        P(None, ("row", "col")),
        P(None, ("row", "col")),
        P(None, ("row", "col")),
        P(None, ("row", "col")),
        P(("row", "col")),
        P(None, ("row", "col")),
        P(("row", "col")),
        P(("row", "col")),
        P(("row", "col")),
        P(("row", "col")),
        P(("row", "col")),
        P(("row", "col"), None),
    )
    return jax.shard_map(
        on_device,
        mesh=mesh,
        in_specs=placed,
        out_specs=(
            P(("dp", "row", "col"), None),
            P(("dp", "row", "col"), None),
            P(),
            P(None, ("row", "col")),
            P(None, ("row", "col")),
            P(None, ("row", "col")),
            P(None, ("row", "col")),
            P(None, ("row", "col")),
            P(("row", "col")),
            P(None, ("row", "col")),
            P(("row", "col")),
            P(("row", "col")),
            P(("row", "col")),
            P(("row", "col")),
            P(("row", "col")),
            P(("row", "col"), None),
        ),
        check_vma=False,
    )
```

```python
from functools import partial

import jax
import jax.numpy as jnp
from jax import lax
from jax.experimental import pallas as pl
from jax.experimental.pallas import tpu as pltpu
from jax.sharding import PartitionSpec as P

HEAD = 64
NS = 128
CONV = 4
BLOCK = 256
LONGEST = 2048
HALO = 16
LANES = 128
EPS = 1e-05
F32 = jnp.float32
BF16 = jnp.bfloat16
HIGHEST = lax.Precision.HIGHEST
RC = ("row", "col")
NT = (((1,), (1,)), ((), ()))
TN = (((0,), (0,)), ((), ()))
VMEM_LIMIT = 56 * 1024 * 1024
BIAS, GAIN, SKIP, TABLE = 4, 5, 6, 8


def dot(a, b, dims=(((1,), (0,)), ((), ()))):
    return lax.dot_general(a, b, dims, preferred_element_type=F32)


def split3(v, lane, heads):
    hi = v.astype(BF16)
    left = v - hi.astype(F32)
    mid = left.astype(BF16)
    lo = (left - mid.astype(F32)).astype(BF16)
    hi, mid, lo = (p.astype(F32) for p in (hi, mid, lo))
    return jnp.where(lane < heads, hi, jnp.where(lane < 2 * heads, mid, lo)).astype(BF16)


def spread(first, width, heads):
    lane = lax.broadcasted_iota(jnp.int32, (LANES, width), 0)
    head = first + lax.broadcasted_iota(jnp.int32, (LANES, width), 1) // HEAD
    hit = (lane == head) | (lane == head + heads) | (lane == head + 2 * heads)
    return jnp.where(hit, 1.0, 0.0).astype(BF16)


def gather_heads(first, width):
    head = first + lax.broadcasted_iota(jnp.int32, (width, LANES), 0) // HEAD
    lane = lax.broadcasted_iota(jnp.int32, (width, LANES), 1)
    return jnp.where(head == lane, 1.0, 0.0).astype(BF16)


def head_sum(v, to_lanes):
    return dot(v.astype(BF16), to_lanes)


def shifted(ext, block, keep):
    start = HALO - 8 + block * BLOCK
    slab = ext[start : start + BLOCK + 8]
    row = lax.broadcasted_iota(jnp.int32, slab.shape, 0)
    slab = jnp.where(row < 8, slab * keep, slab)
    return [slab[8:]] + [pltpu.roll(slab, o, 0)[8:] for o in range(1, CONV)]


def conv_rows(parts, taps, bias):
    total = parts[0] * taps[CONV - 1 : CONV] + bias
    for o in range(1, CONV):
        total = total + parts[o] * taps[CONV - 1 - o : CONV - o]
    return total


def sigmoid(v):
    return 1.0 / (1.0 + jnp.exp(-v))


def conv_back(d_sum, taps):
    zero = jnp.zeros((8, d_sum.shape[1]), F32)
    slab = jnp.concatenate([zero, d_sum, zero], axis=0)
    rows = slab.shape[0]
    total = slab * taps[CONV - 1 : CONV]
    for o in range(1, CONV):
        total = total + pltpu.roll(slab, rows - o, 0) * taps[CONV - 1 - o : CONV - o]
    return total[: BLOCK + 8]


def prep_kernel(
    blocks, heads,
    flags, nx, wbd, taps, bias, dt_bias, rate,
    bc_pre_o, b_o, c_o, bt_o, ct_o, raw_o, dt_o, dtp_o, cum_o, cump_o, cumt_o,
):
    pre = dot(nx[...], wbd[...], NT).astype(BF16)
    bc_pre_o[...] = pre[:, : 2 * NS]
    ext = pre[:, : 2 * NS].astype(F32)
    raw = pre[HALO:, 2 * NS :].astype(F32) + dt_bias[...]
    raw_o[...] = raw
    step = jnp.maximum(raw, 0.0) + jnp.log1p(jnp.exp(-jnp.abs(raw)))
    lane = lax.broadcasted_iota(jnp.int32, step.shape, 1)
    dt_o[...] = step
    dtp_o[...] = split3(jnp.where(lane < 3 * heads, step, 0.0), lane, heads)
    scaled = step * rate[...]
    tri = jnp.where(
        lax.broadcasted_iota(jnp.int32, (BLOCK, BLOCK), 0)
        >= lax.broadcasted_iota(jnp.int32, (BLOCK, BLOCK), 1),
        1.0,
        0.0,
    )
    for b in range(blocks):
        at = slice(b * BLOCK, (b + 1) * BLOCK)
        cum = jnp.dot(tri, scaled[at], precision=HIGHEST, preferred_element_type=F32)
        cum_o[at, :] = cum
        cump_o[at, :] = split3(cum, lane[at], heads)
        cumt_o[:, at] = cum.T
        conv = conv_rows(shifted(ext, b, flags[b]), taps[...], bias[...])
        bc = (conv * sigmoid(conv)).astype(BF16)
        b_o[at, :] = bc[:, :NS]
        c_o[at, :] = bc[:, NS:]
        bc32 = bc.astype(F32)
        bt_o[:, at] = bc32[:, :NS].T.astype(BF16)
        ct_o[:, at] = bc32[:, NS:].T.astype(BF16)


def state_kernel(
    blocks, heads,
    flags, nx, w, w_other, table, dtp, cump, bt,
    pre_o, x_o, hloc_o, sent_o, fade_o,
):
    g = pl.program_id(0)
    width = x_o.shape[1]
    own = g % 2 == flags[2 * blocks].astype(jnp.int32)
    pre = dot(nx[...], jnp.where(own, w[0], w_other[0])).astype(BF16)
    pre_o[...] = pre
    ext = pre.astype(F32)
    to_cols = spread(g * (width // HEAD), width, heads)
    dt = dot(dtp[...], to_cols)
    cum = dot(cump[...], to_cols)
    carried = jnp.zeros((NS, width), F32)
    through = jnp.ones((1, width), F32)
    for b in range(blocks):
        at = slice(b * BLOCK, (b + 1) * BLOCK)
        conv = conv_rows(shifted(ext, b, flags[b]), table[:CONV], table[BIAS : BIAS + 1])
        x = conv * sigmoid(conv)
        x_o[at, :] = x.astype(BF16)
        cum_b = cum[at]
        last = cum_b[BLOCK - 1 : BLOCK]
        tail = (x * dt[at] * jnp.exp(last - cum_b)).astype(BF16)
        fade = jnp.exp(last)
        carried = carried * flags[b]
        through = through * flags[b]
        hloc_o[b] = carried.astype(BF16)
        fade_o[b : b + 1, :] = through
        fade_o[blocks + b : blocks + b + 1, :] = fade
        carried = fade * carried + dot(bt[:, at], tail)
        through = through * fade
    sent_o[:NS, :] = carried.astype(BF16)
    sent_o[NS:, :] = jnp.broadcast_to(through, (sent_o.shape[0] - NS, width)).astype(BF16)


def head_column(cum, head):
    lane = lax.broadcasted_iota(jnp.int32, cum.shape, 1)
    return jnp.sum(jnp.where(lane == head, cum, 0.0), axis=1, keepdims=True)


def stacked(v, count):
    head = lax.broadcasted_iota(jnp.int32, v.shape, 1) // HEAD
    return jnp.concatenate(
        [jnp.where(head == i, v, 0.0).astype(BF16) for i in range(count)], axis=0
    )


def inner_kernel(blocks, heads, table, b_in, c_in, x_in, dtp, cum_in, cumt_in, y_o, scores):
    g = pl.program_id(0)
    width = y_o.shape[1]
    count = width // HEAD

    @pl.when(g == 0)
    def _():
        for b in range(blocks):
            at = slice(b * BLOCK, (b + 1) * BLOCK)
            scores[b] = dot(c_in[at, :], b_in[at, :], NT)

    dt = dot(dtp[...], spread(g * count, width, heads))
    lower = lax.broadcasted_iota(jnp.int32, (BLOCK, BLOCK), 0) >= lax.broadcasted_iota(
        jnp.int32, (BLOCK, BLOCK), 1
    )
    for b in range(blocks):
        at = slice(b * BLOCK, (b + 1) * BLOCK)
        x = x_in[at, :].astype(F32)
        u = stacked(x * dt[at], count)
        cum = cum_in[at, :]
        weights = []
        for i in range(count):
            h = g * count + i
            diff = head_column(cum, h) - cumt_in[pl.ds(h, 1), at]
            decay = jnp.exp(jnp.where(lower, diff, -1e30))
            weights.append((scores[b] * decay).astype(BF16))
        y = dot(jnp.concatenate(weights, axis=1), u)
        y_o[at, :] = (y + x * table[SKIP : SKIP + 1]).astype(BF16)


def project_kernel(nx, d_mix, w, z_o, back_o):
    width = z_o.shape[1]
    z_o[...] = dot(nx[HALO:, :], w[0, :width], NT).astype(BF16)
    back_o[...] = dot(d_mix[...], w[0, width:], NT).astype(BF16)


def middle_kernel(
    heads,
    table, y_in, z_in, x_in, back_in, c_in, ct_in, cump, hloc, before, fade,
    yout_o, dy_o, dz_o, row_o, dc_o, dst_o, sums_o, sent_o,
):
    b = pl.program_id(0)
    width = y_in.shape[1]
    through = fade[pl.ds(b, 1), :]
    enter = (through * before[:NS].astype(F32) + hloc[0].astype(F32)).astype(BF16)
    grow = jnp.exp(dot(cump[...], spread(0, width, heads)))
    across = dot(c_in[...], enter) * grow
    y = y_in[...].astype(F32) + across
    z = z_in[...].astype(F32)
    gate = sigmoid(z)
    silu = z * gate
    gated = y * silu
    rs = lax.rsqrt(jnp.sum(gated * gated, axis=1, keepdims=True) / width + EPS)
    unit = gated * rs
    gain = table[GAIN : GAIN + 1]
    yout_o[...] = (unit * gain).astype(BF16)
    back = back_in[...].astype(F32)
    d_unit = back * gain
    along = jnp.sum(d_unit * gated, axis=1, keepdims=True) / width
    d_gated = rs * d_unit - gated * (rs * rs * rs * along)
    dy = d_gated * silu
    dy_o[...] = dy.astype(BF16)
    dz_o[...] = (d_gated * y * (gate * (1.0 + z * (1.0 - gate)))).astype(BF16)
    row_o[...] = head_sum(dy * across, gather_heads(0, width))
    grown = (dy * grow).astype(BF16)
    dc_o[...] = dot(grown, enter, NT)
    dst = dot(ct_in[...], grown)
    dst_o[0] = dst.astype(BF16)

    @pl.when(b == 0)
    def _():
        sums_o[...] = jnp.zeros_like(sums_o)
        sent_o[...] = jnp.zeros_like(sent_o)

    sums_o[0:1] += jnp.sum(back * unit, axis=0, keepdims=True)
    sums_o[1:2] += jnp.sum(dy * x_in[...].astype(F32), axis=0, keepdims=True)
    sent_o[...] += through * dst


def weights_kernel(blocks, flags, nx, d_mix, dz, yout, keep_o, give_o):
    g = pl.program_id(0)
    width = dz.shape[1]
    own = g % 2 == flags[2 * blocks].astype(jnp.int32)
    dw_z = dot(dz[...], nx[HALO:, :], TN).astype(BF16)
    dw_out = dot(yout[...], d_mix[...], TN).astype(BF16)

    @pl.when(own)
    def _():
        keep_o[0, :width] = dw_z
        keep_o[0, width:] = dw_out

    @pl.when(jnp.logical_not(own))
    def _():
        give_o[0, :width] = dw_z
        give_o[0, width:] = dw_out


def mix_kernel(blocks, flags, w, dz, yout, x_rows, dn_o, out_o):
    inner = dz.shape[1]
    width = inner // w.shape[0]
    tile = out_o.shape[1]
    dn_o[...] = dot(dz[...], w[:, :width, :].reshape(inner, tile))
    mix = dot(yout[...], w[:, width:, :].reshape(inner, tile))
    for b in range(blocks):
        at = slice(b * BLOCK, (b + 1) * BLOCK)
        live = flags[blocks + b]
        out_o[at, :] = (x_rows[at, :].astype(F32) + live * mix[at]).astype(BF16)


def norm_back_kernel(blocks, flags, w, w_other, d_pre_a, d_pre_b, dn_z, dn_o):
    first = flags[2 * blocks] == 0.0
    members = []
    for z in range(w.shape[0]):
        members += [jnp.where(first, w[z], w_other[z]), jnp.where(first, w_other[z], w[z])]
    half = len(members) // 2
    total = dot(d_pre_a[...], jnp.concatenate(members[:half], axis=1), NT)
    total += dot(d_pre_b[...], jnp.concatenate(members[half:], axis=1), NT)
    dn_o[:HALO, :] = total[:HALO]
    dn_o[HALO:, :] = total[HALO:] + dn_z[...]


def inner_back_kernel(
    blocks, heads,
    b_in, c_in, x_in, dy_in, dtp, cum_in, cumt_in,
    du_o, dbc_o, rows_o, cols_o, scores, d_scores,
):
    g = pl.program_id(0)
    width = du_o.shape[1]
    count = width // HEAD

    @pl.when(g == 0)
    def _():
        d_scores[...] = jnp.zeros_like(d_scores)
        cols_o[...] = jnp.zeros_like(cols_o)
        for b in range(blocks):
            at = slice(b * BLOCK, (b + 1) * BLOCK)
            scores[b] = dot(b_in[at, :], c_in[at, :], NT)

    rows_o[...] = jnp.zeros_like(rows_o)
    dt = dot(dtp[...], spread(g * count, width, heads))
    lower = lax.broadcasted_iota(jnp.int32, (BLOCK, BLOCK), 0) <= lax.broadcasted_iota(
        jnp.int32, (BLOCK, BLOCK), 1
    )
    for b in range(blocks):
        at = slice(b * BLOCK, (b + 1) * BLOCK)
        u = (x_in[at, :].astype(F32) * dt[at]).astype(BF16)
        dy = stacked(dy_in[at, :].astype(F32), count)
        d_w = dot(u, dy, NT)
        cum = cum_in[at, :]
        lane = lax.broadcasted_iota(jnp.int32, cum.shape, 1)
        cols = cols_o[at, :]
        weights = []
        for i in range(count):
            h = g * count + i
            diff = cumt_in[pl.ds(h, 1), at] - head_column(cum, h)
            decay = jnp.exp(jnp.where(lower, diff, -1e30))
            weights.append((scores[b] * decay).astype(BF16))
            d_score = d_w[:, i * BLOCK : (i + 1) * BLOCK] * decay
            d_scores[b] += d_score
            both = d_score * scores[b]
            rows_o[0, i : i + 1, at] = jnp.sum(both, axis=0, keepdims=True)
            cols = jnp.where(lane == h, jnp.sum(both, axis=1, keepdims=True), cols)
        cols_o[at, :] = cols
        du_o[at, :] = dot(jnp.concatenate(weights, axis=1), dy).astype(BF16)

    @pl.when(g == pl.num_programs(0) - 1)
    def _():
        for b in range(blocks):
            at = slice(b * BLOCK, (b + 1) * BLOCK)
            ds = d_scores[b].astype(BF16)
            dbc_o[at, :NS] = dot(ds, c_in[at, :])
            dbc_o[at, NS:] = dot(ds, b_in[at, :], TN)


def back_kernel(
    blocks, heads, base,
    flags, db_in, q_in, gdt_in, nx_t, table, pre_in, dy_in, du_in, b_in, dtp, cump, hloc, before, after, dst, fade,
    keep_o, give_o, d_pre_o, db_o, q_o, gdt_o, fdh_o, dtap_o, d_ext,
):
    g = pl.program_id(0)
    width = dy_in.shape[1]
    first = (base + g) * (width // HEAD)

    @pl.when(g == 0)
    def _():
        db_o[...] = db_in[...]
        q_o[...] = q_in[...]
        gdt_o[...] = gdt_in[...]

    to_cols = spread(first, width, heads)
    to_lanes = gather_heads(first, width)
    dt_all = dot(dtp[...], to_cols)
    cum_all = dot(cump[...], to_cols)
    ext = pre_in[...].astype(F32)
    taps = table[:CONV]
    skip = table[SKIP : SKIP + 1]
    d_states = [None] * blocks
    d_state = after[:NS].astype(F32)
    for b in reversed(range(blocks)):
        d_states[b] = d_state
        fade_b = fade[blocks + b : blocks + b + 1]
        d_state = flags[b] * (fade_b * d_state + dst[b].astype(F32))
    d_ext[:HALO, :] = jnp.zeros((HALO, width), F32)
    d_taps = [jnp.zeros((1, width), F32) for _ in range(CONV + 1)]
    fdh_o[...] = jnp.zeros_like(fdh_o)
    for b in range(blocks):
        at = slice(b * BLOCK, (b + 1) * BLOCK)
        enter = fade[b : b + 1] * before[:NS].astype(F32) + hloc[b].astype(F32)
        fdh_o[b : b + 1, :] = fade[blocks + b : blocks + b + 1] * jnp.sum(
            enter * d_states[b], axis=0, keepdims=True
        )
        d_st = d_states[b].astype(BF16)
        parts = shifted(ext, b, flags[b])
        conv = conv_rows(parts, taps, table[BIAS : BIAS + 1])
        sig = sigmoid(conv)
        x = conv * sig
        dt = dt_all[at]
        cum = cum_all[at]
        tail = jnp.exp(cum[BLOCK - 1 : BLOCK] - cum)
        u = x * dt
        du_state = dot(b_in[at, :], d_st) * tail
        du = du_in[at, :].astype(F32) + du_state
        db_o[at, :] += dot((u * tail).astype(BF16), d_st, NT)
        q_o[at, :] += head_sum(u * du_state, to_lanes)
        gdt_o[at, :] += head_sum(x * du, to_lanes)
        dx = dt * du + skip * dy_in[at, :].astype(F32)
        d_sum = dx * (sig * (1.0 + conv * (1.0 - sig)))
        for o in range(CONV):
            d_taps[CONV - 1 - o] += jnp.sum(d_sum * parts[o], axis=0, keepdims=True)
        d_taps[CONV] += jnp.sum(d_sum, axis=0, keepdims=True)
        carried = conv_back(d_sum, taps)
        start = HALO + b * BLOCK
        d_ext[start - 8 : start, :] += flags[b] * carried[:8]
        d_ext[start : start + BLOCK, :] = carried[8:]
    dtap_o[...] = jnp.concatenate(d_taps + [jnp.zeros((3, width), F32)], axis=0)
    d_pre = d_ext[...].astype(BF16)
    d_pre_o[...] = d_pre
    dw = dot(nx_t[...], d_pre).astype(BF16)
    own = g % 2 == flags[2 * blocks].astype(jnp.int32)

    @pl.when(own)
    def _():
        keep_o[0] = dw

    @pl.when(jnp.logical_not(own))
    def _():
        give_o[0] = dw


def last_kernel(
    blocks, heads,
    flags, nx, wbd, taps_in, bias, rate, bc_pre, dbc, dc, db, raw, step_in,
    rows, cols, row, q, gdt, fdh, dn_x, x_ext, rstd,
    dw_o, dn_o, gain_o, dtap_o, ddt_o, d_ext,
):
    taps = taps_in[...]
    ext = bc_pre[...].astype(F32)
    width = ext.shape[1]
    d_ext[:HALO, :] = jnp.zeros((HALO, d_ext.shape[1]), F32)
    d_taps = [jnp.zeros((1, width), F32) for _ in range(CONV + 1)]
    bias_sum = jnp.zeros((1, LANES), F32)
    rate_sum = jnp.zeros((1, LANES), F32)
    row_i = lax.broadcasted_iota(jnp.int32, (BLOCK, BLOCK), 0)
    col_i = lax.broadcasted_iota(jnp.int32, (BLOCK, BLOCK), 1)
    onward = jnp.where(row_i <= col_i, 1.0, 0.0)
    earlier = jnp.where(row_i > col_i, 1.0, 0.0)
    lane = lax.broadcasted_iota(jnp.int32, (BLOCK, LANES), 1)
    faded = jnp.dot(
        fdh[...], gather_heads(0, fdh.shape[1]).astype(F32), precision=HIGHEST,
        preferred_element_type=F32,
    )
    for b in range(blocks):
        at = slice(b * BLOCK, (b + 1) * BLOCK)
        start = HALO + b * BLOCK
        flow = rows[at, :] - cols[at, :] + row[at, :]
        d_a = (
            jnp.dot(onward, flow, precision=HIGHEST, preferred_element_type=F32)
            + jnp.dot(earlier, q[at, :], precision=HIGHEST, preferred_element_type=F32)
            + faded[b : b + 1]
        )
        step = step_in[at, :]
        d_step = gdt[at, :] + rate[...] * d_a
        d_raw = jnp.where(lane < heads, d_step * sigmoid(raw[at, :]), 0.0)
        bias_sum += jnp.sum(d_raw, axis=0, keepdims=True)
        rate_sum += jnp.sum(step * d_a, axis=0, keepdims=True)
        d_ext[start : start + BLOCK, 2 * NS :] = d_raw
        parts = shifted(ext, b, flags[b])
        conv = conv_rows(parts, taps, bias[...])
        sig = sigmoid(conv)
        d_bc = dbc[at, :] + jnp.concatenate([db[at, :], dc[at, :]], axis=1)
        d_sum = d_bc * (sig * (1.0 + conv * (1.0 - sig)))
        for o in range(CONV):
            d_taps[CONV - 1 - o] += jnp.sum(d_sum * parts[o], axis=0, keepdims=True)
        d_taps[CONV] += jnp.sum(d_sum, axis=0, keepdims=True)
        carried = conv_back(d_sum, taps)
        d_ext[start - 8 : start, : 2 * NS] += flags[b] * carried[:8]
        d_ext[start : start + BLOCK, : 2 * NS] = carried[8:]
    dtap_o[...] = jnp.concatenate(d_taps + [jnp.zeros((3, width), F32)], axis=0)
    ddt_o[...] = jnp.concatenate(
        [bias_sum, rate_sum * rate[...], jnp.zeros((6, LANES), F32)], axis=0
    )
    d_pre = d_ext[...].astype(BF16)
    dw_o[...] = dot(d_pre, nx[...], TN).astype(BF16)
    total = dn_x[...] + dot(d_pre, wbd[...])
    dn_o[...] = total
    gain_o[...] = jnp.sum(total * (x_ext[...].astype(F32) * rstd[...]), axis=0, keepdims=True)


def whole(shape):
    rank = len(shape)
    return pl.BlockSpec(shape, lambda *_: (0,) * rank)


SMEM = pl.BlockSpec(memory_space=pltpu.SMEM)


def cols_of(rows, width):
    return pl.BlockSpec((rows, width), lambda g: (0, g))


def member_of(rows, width):
    return pl.BlockSpec((1, rows, width), lambda g: (g, 0, 0))


def pair_of(rows, width):
    return pl.BlockSpec((1, rows, width), lambda g: (g // 2, 0, 0))


def call(kernel, grid, ins, outs, scratch, name, us, *args, after=()):
    count = len(args)

    def body(*refs):
        kernel(*refs[:count], *refs[count + len(after) :])

    return pl.pallas_call(
        body,
        grid=grid,
        in_specs=list(ins) + [pl.BlockSpec(memory_space=pl.ANY)] * len(after),
        out_specs=[spec for _, _, spec in outs],
        out_shape=[jax.ShapeDtypeStruct(shape, dtype) for shape, dtype, _ in outs],
        scratch_shapes=scratch,
        compiler_params=pltpu.CompilerParams(vmem_limit_bytes=VMEM_LIMIT),
        cost_estimate=pl.CostEstimate(
            flops=int(us * 1.1e9), bytes_accessed=int(us * 1e6), transcendentals=0
        ),
        name=name,
    )(*args, *after)


def state_scan(own, members, tokens, forward, beside=()):
    def moved(v, by):
        pairs = [(i, i + by) for i in range(members - by)]
        if not forward:
            pairs = [(b, a) for a, b in pairs]
        return lax.ppermute(v, RC, pairs)

    reach = min(members - 1, -(-LONGEST // tokens))
    is_term = lax.broadcasted_iota(jnp.int32, own.shape, 0) < NS
    steps = []
    span = 1
    while span < reach:
        got = moved(own, span).astype(F32)
        if len(steps) < len(beside):
            own, _ = lax.optimization_barrier((own, beside[len(steps)]))
        held = own.astype(F32)
        own = (jnp.where(is_term, held, 0.0) + held[NS : NS + 1] * got).astype(BF16)
        steps.append(own)
        span *= 2
    steps.append(moved(own, 1))
    return steps


def thrice(v):
    hi = lax.optimization_barrier(v.astype(BF16))
    left = v - hi.astype(F32)
    mid = lax.optimization_barrier(left.astype(BF16))
    lo = (left - mid.astype(F32)).astype(BF16)
    return jnp.stack([hi, mid, lo])


def halves(v, axis):
    half = v.shape[axis] // 2
    return lax.slice_in_dim(v, 0, half, axis=axis), lax.slice_in_dim(v, half, None, axis=axis)


def dp_bits():
    return [1 << i for i in range((lax.axis_size("dp") - 1).bit_length())]


def across_dp(v, bit):
    return lax.ppermute(v, "dp", [(i, i ^ bit) for i in range(lax.axis_size("dp"))])


def set_bit(bit):
    return (lax.axis_index("dp") // bit) % 2 == 1


def gather_dp(v, axis):
    bits = dp_bits()
    me = lax.axis_index("dp")
    for low in range(0, len(bits), 2):
        count = 1 << len(bits[low : low + 2])
        mine = (me // bits[low]) % count
        size = v.shape[axis]
        shape = list(v.shape)
        shape[axis] = size * count
        out = jnp.zeros(shape, v.dtype)
        for by in range(count):
            piece = across_dp(v, by * bits[low]) if by else v
            out = lax.dynamic_update_slice_in_dim(out, piece, (mine ^ by) * size, axis)
        v = out
    return v


def double(v, bit, axis):
    got = across_dp(v, bit)
    up = set_bit(bit)
    return jnp.concatenate([jnp.where(up, got, v), jnp.where(up, v, got)], axis=axis)


def doubled(v, bits, axis):
    for bit in bits:
        v = double(v, bit, axis)
    return v


def to_halve(v, bit, axis):
    low, high = halves(v, axis)
    up = set_bit(bit)
    return jnp.where(up, high, low), jnp.where(up, low, high)


def summed(stays, goes, bit):
    return (stays.astype(F32) + across_dp(goes, bit).astype(F32)).astype(BF16)


def along_row(v, by):
    rows = lax.axis_size("row")
    return lax.ppermute(v, "row", [(i, (i + by) % rows) for i in range(rows)])


def other_col(v):
    return lax.ppermute(v, "col", [(0, 1), (1, 0)])


def gather_rows(v):
    rows = lax.axis_size("row")
    row = lax.axis_index("row")
    out = jnp.zeros((rows,) + v.shape, v.dtype)
    for by in range(rows):
        piece = v if by == 0 else along_row(v, by)
        out = lax.dynamic_update_index_in_dim(out, piece, (row - by) % rows, 0)
    return out


def row_pieces(v):
    rows = lax.axis_size("row")
    row = lax.axis_index("row")
    return tuple(
        lax.dynamic_index_in_dim(v, (row + by) % rows, 0, keepdims=False) for by in range(rows)
    )


def sum_rows(pieces):
    terms = [(p if by == 0 else along_row(p, by)).astype(F32) for by, p in enumerate(pieces)]
    while len(terms) > 1:
        half = len(terms) // 2
        terms = [terms[i] + terms[i + half] for i in range(half)]
    return terms[0]


def reduce_shards(parts):
    bits = dp_bits()
    sums = [(k.astype(F32) + other_col(v).astype(F32)).astype(BF16) for k, v in parts]
    now = halves(jnp.concatenate(sums, axis=0), 1)
    for one, two in zip(bits[::-1], bits):
        a, b, c, d = yield to_halve(now[0], one, 1) + to_halve(now[1], two, 1)
        now = summed(a, b, one), summed(c, d, two)
    cut = now[0].shape[1]
    pieces = yield row_pieces(jnp.concatenate(now, axis=1))
    (part,) = yield (sum_rows(pieces).astype(BF16),)
    n = lax.axis_size("dp")
    whole_sum = gather_dp(part[None], 0)
    first = whole_sum[:, :cut]
    second = whole_sum[:, cut:]
    count = len(bits)
    shape = second.shape
    second = second.reshape((2,) * count + shape[1:])
    second = second.transpose(tuple(reversed(range(count))) + (count, count + 1)).reshape(shape)
    yield (first.reshape(n * cut, -1), second.reshape(n * cut, -1))


def reduce_small(v):
    even, odd = v[:, 0], v[:, 1]
    first = lax.axis_index("col") == 0
    both = jnp.where(first, even, odd).astype(F32) + other_col(
        jnp.where(first, odd, even)
    ).astype(F32)
    pieces = yield row_pieces(both.astype(BF16))
    now = yield (sum_rows(pieces),)
    for bit in dp_bits():
        now = yield (now[0] + across_dp(now[0], bit),)


def in_step(runs, states):
    running = list(range(len(runs)))
    while running:
        left = []
        for i in running:
            try:
                states[i] = next(runs[i]) if states[i] is None else runs[i].send(states[i])
                left.append(i)
            except StopIteration:
                pass
        running = left
        if running:
            tied = lax.optimization_barrier([states[i] for i in running])
            for i, value in zip(running, tied):
                states[i] = value
    return states


def gather_shards(v):
    bits = dp_bits()
    me = lax.axis_index("dp")
    turned = sum(((me // bit) % 2) * back for bit, back in zip(bits, bits[::-1]))
    first, second = halves(v, 0)
    rows = first.shape[0] // lax.axis_size("dp")
    mine = jnp.concatenate(
        [lax.dynamic_slice_in_dim(first, me * rows, rows, 0),
         lax.dynamic_slice_in_dim(second, turned * rows, rows, 0)], axis=0
    )
    got = gather_rows(mine)
    first = doubled(got[:, :rows], bits, 1)
    second = doubled(got[:, rows:], bits[::-1], 1)
    own = jnp.concatenate([first, second], axis=1)
    return own, other_col(own)


def on_device(
    block_input, d_out, lengths, gain_in, w_z, w_x, w_bc, w_dt, conv_x, conv_x_bias,
    conv_bc, conv_bc_bias, dt_bias, a_log, d_skip, gain_gate, w_out,
):
    members = lax.axis_size(RC)
    place = lax.axis_index(RC)
    tokens, model = block_input.shape
    blocks = tokens // BLOCK
    width = w_x.shape[1]
    inner = width * members
    group_heads = w_dt.shape[1]
    heads = group_heads * members
    bc_cols = w_bc.shape[1]
    ext_rows = tokens + HALO

    small = jnp.concatenate(
        [conv_x.reshape(-1), conv_x_bias, gain_gate, conv_bc.reshape(-1), conv_bc_bias,
         dt_bias, a_log, d_skip]
    )
    small_rows = -(-small.shape[0] // model)
    parts = thrice(jnp.pad(small, (0, small_rows * model - small.shape[0])))
    side = bc_cols + group_heads
    rows1 = side + 3 * small_rows
    pack1 = jnp.concatenate(
        [w_bc.T, w_dt.T, parts.reshape(3 * small_rows, model),
         jnp.zeros((-rows1 % 16, model), BF16)], axis=0
    )
    col = lax.axis_index("col")
    own1 = gather_rows(pack1)
    other1 = other_col(own1)
    all1 = jnp.where(
        col == 0, jnp.stack([own1, other1], axis=1), jnp.stack([other1, own1], axis=1)
    ).reshape(members, -1, model)
    wx_own, wx_other = gather_shards(w_x)
    pack2 = jnp.concatenate([w_z.T, w_out], axis=0)
    all2 = lax.all_gather(pack2, RC, axis=0)

    ends = jnp.cumsum(lengths[0])
    firsts = jnp.arange(members * blocks, dtype=jnp.int32) * BLOCK

    def segment(at):
        return jnp.sum((at[:, None] >= ends[None, :]).astype(jnp.int32), axis=1)

    kept = (segment(firsts) == segment(firsts - 1)) & (firsts > 0)
    both = jnp.stack([kept, firsts < ends[-1]]).astype(F32)
    flags = lax.dynamic_slice(both, (0, place * blocks), (2, blocks)).reshape(-1)
    flags = jnp.concatenate([flags, col.astype(F32)[None]])

    ahead = [(i, i + 1) for i in range(members - 1)]
    back = [(i + 1, i) for i in range(members - 1)]
    tail_rows = lax.ppermute(block_input[tokens - HALO :], RC, ahead)
    x_ext = jnp.concatenate([tail_rows, block_input], axis=0)
    x32 = x_ext.astype(F32)
    rstd = lax.rsqrt(jnp.mean(x32 * x32, axis=1, keepdims=True) + EPS)
    nx = (x32 * rstd * gain_in).astype(BF16)
    nx_t = nx.T
    live = jnp.repeat(flags[blocks : 2 * blocks], BLOCK)[:, None]
    d_mix = (d_out.astype(F32) * live).astype(BF16)

    w_bc_t = all1[:, :bc_cols].reshape(-1, model)
    w_dt_t = all1[:, bc_cols:side].reshape(-1, model)
    wbd = jnp.concatenate(
        [w_bc_t, w_dt_t, w_dt_t, w_dt_t, jnp.zeros((LANES - 3 * heads, model), BF16)], axis=0
    )
    pieces = all1[:, side : side + 3 * small_rows].astype(F32)
    pieces = pieces.reshape(members, 3, small_rows * model)
    small_all = pieces[:, 0] + pieces[:, 1] + pieces[:, 2]
    sizes = [conv_x.size, width, width, conv_bc.size, bc_cols, group_heads, group_heads, group_heads]
    cuts = [sum(sizes[:i]) for i in range(len(sizes) + 1)]
    s_conv, s_bias, s_gain, s_cbc, s_cbias, s_dtb, s_alog, s_skip = (
        small_all[:, cuts[i] : cuts[i + 1]] for i in range(len(sizes))
    )
    skip_cols = jnp.repeat(s_skip.reshape(-1), HEAD)[None]
    table = jnp.concatenate(
        [s_conv.reshape(members, CONV, width).transpose(1, 0, 2).reshape(CONV, inner),
         s_bias.reshape(1, inner), s_gain.reshape(1, inner), skip_cols,
         jnp.zeros((1, inner), F32)], axis=0
    )
    taps_bc = s_cbc.reshape(members, CONV, bc_cols).transpose(1, 0, 2).reshape(CONV, 2 * NS)
    bias_bc = s_cbias.reshape(1, 2 * NS)

    def lanes(v):
        return jnp.pad(jnp.tile(v.reshape(1, heads), (1, 3)), ((0, 0), (0, LANES - 3 * heads)))

    dtb = lanes(s_dtb)
    rate = lanes(-jnp.exp(s_alog))

    (bc_pre, b16, c16, bt, ct, raw, step, dtp, cum, cump, cumt) = call(
        partial(prep_kernel, blocks, heads), (1,),
        [SMEM, whole((ext_rows, model)), whole(wbd.shape), whole(taps_bc.shape),
         whole(bias_bc.shape), whole((1, LANES)), whole((1, LANES))],
        [((ext_rows, 2 * NS), BF16, whole((ext_rows, 2 * NS))),
         ((tokens, NS), BF16, whole((tokens, NS))),
         ((tokens, NS), BF16, whole((tokens, NS))),
         ((NS, tokens), BF16, whole((NS, tokens))),
         ((NS, tokens), BF16, whole((NS, tokens))),
         ((tokens, LANES), F32, whole((tokens, LANES))),
         ((tokens, LANES), F32, whole((tokens, LANES))),
         ((tokens, LANES), BF16, whole((tokens, LANES))),
         ((tokens, LANES), F32, whole((tokens, LANES))),
         ((tokens, LANES), BF16, whole((tokens, LANES))),
         ((LANES, tokens), F32, whole((LANES, tokens)))],
        [], "prep", 4, flags, nx, wbd, taps_bc, bias_bc, dtb, rate,
    )
    lane_rows = whole((tokens, LANES))
    sent_rows = NS + 16
    x_pre, x16, hloc, own, fade = call(
        partial(state_kernel, blocks, heads), (members,),
        [SMEM, whole((ext_rows, model)), pair_of(model, width), pair_of(model, width),
         cols_of(TABLE, width), lane_rows, lane_rows, whole((NS, tokens))],
        [((ext_rows, inner), BF16, cols_of(ext_rows, width)),
         ((tokens, inner), BF16, cols_of(tokens, width)),
         ((blocks, NS, inner), BF16, pl.BlockSpec((blocks, NS, width), lambda g: (0, 0, g))),
         ((sent_rows, inner), BF16, cols_of(sent_rows, width)),
         ((2 * blocks, inner), F32, cols_of(2 * blocks, width))],
        [], "states", 12, flags, nx, wx_own, wx_other, table, dtp, cump, bt,
    )
    before = state_scan(own, members, tokens, True)[-1]
    (y_loc,) = call(
        partial(inner_kernel, blocks, heads), (members,),
        [cols_of(TABLE, width), whole((tokens, NS)), whole((tokens, NS)), cols_of(tokens, width),
         lane_rows, lane_rows, whole((LANES, tokens))],
        [((tokens, inner), BF16, cols_of(tokens, width))],
        [pltpu.VMEM((blocks, BLOCK, BLOCK), F32)], "inner", 9,
        table, b16, c16, x16, dtp, cum, cumt,
    )
    z_pre, d_yout = call(
        project_kernel, (members,),
        [whole((ext_rows, model)), whole((tokens, model)), member_of(2 * width, model)],
        [((tokens, inner), BF16, cols_of(tokens, width))] * 2,
        [], "project", 11, nx, d_mix, all2,
    )

    def rows_of(cols):
        return pl.BlockSpec((BLOCK, cols), lambda b: (b, 0))

    y_out, dy, dz, row, dc, dst, sums, grad_own = call(
        partial(middle_kernel, heads), (blocks,),
        [whole((TABLE, inner)), rows_of(inner), rows_of(inner), rows_of(inner), rows_of(inner),
         rows_of(NS), pl.BlockSpec((NS, BLOCK), lambda b: (0, b)), rows_of(LANES),
         pl.BlockSpec((1, NS, inner), lambda b: (b, 0, 0)), whole((sent_rows, inner)),
         whole((2 * blocks, inner))],
        [((tokens, inner), BF16, rows_of(inner)),
         ((tokens, inner), BF16, rows_of(inner)),
         ((tokens, inner), BF16, rows_of(inner)),
         ((tokens, LANES), F32, rows_of(LANES)),
         ((tokens, NS), F32, rows_of(NS)),
         ((blocks, NS, inner), BF16, pl.BlockSpec((1, NS, inner), lambda b: (b, 0, 0))),
         ((8, inner), F32, whole((8, inner))),
         ((NS, inner), F32, whole((NS, inner)))],
        [], "middle", 14, table, y_loc, z_pre, x16, d_yout, c16, ct, cump, hloc, before, fade,
    )
    (keep2, give2) = call(
        partial(weights_kernel, blocks), (members,),
        [SMEM, whole((ext_rows, model)), whole((tokens, model)),
         cols_of(tokens, width), cols_of(tokens, width)],
        [((members // 2, 2 * width, model), BF16, pair_of(2 * width, model)),
         ((members // 2, 2 * width, model), BF16, pair_of(2 * width, model))],
        [], "weights", 10, flags, nx, d_mix, dz, y_out,
    )
    grad_own = jnp.concatenate([grad_own.astype(BF16), own[NS:]], axis=0)
    scan = state_scan(grad_own, members, tokens, False, (keep2,))
    give2, _ = lax.optimization_barrier((give2, scan[0]))
    run2 = reduce_shards([(keep2, give2)])
    tile = model // 4
    state2 = next(run2)
    du, dbc, rows, cols = call(
        partial(inner_back_kernel, blocks, heads), (members,),
        [whole((tokens, NS)), whole((tokens, NS)), cols_of(tokens, width), cols_of(tokens, width),
         lane_rows, lane_rows, whole((LANES, tokens))],
        [((tokens, inner), BF16, cols_of(tokens, width)),
         ((tokens, 2 * NS), F32, whole((tokens, 2 * NS))),
         ((members, 8, tokens), F32, member_of(8, tokens)),
         ((tokens, LANES), F32, lane_rows)],
        [pltpu.VMEM((blocks, BLOCK, BLOCK), F32), pltpu.VMEM((blocks, BLOCK, BLOCK), F32)],
        "inner_back", 12, b16, c16, x16, dy, dtp, cum, cumt, after=(scan[0], keep2),
    )
    dn_z, block_out = call(
        partial(mix_kernel, blocks), (4,),
        [SMEM, pl.BlockSpec((members, 2 * width, tile), lambda n: (0, 0, n)),
         whole((tokens, inner)), whole((tokens, inner)), cols_of(tokens, tile)],
        [((tokens, model), F32, cols_of(tokens, tile)),
         ((tokens, model), BF16, cols_of(tokens, tile))],
        [], "mix", 9, flags, all2, dz, y_out, block_input, after=(scan[-2], du) + state2,
    )
    after = scan[-1]
    rows = jnp.pad(
        rows[:, :group_heads].reshape(heads, tokens).T, ((0, 0), (0, LANES - heads))
    )
    half = members // 2

    def run_back(base, sums_in, waits):
        def at(rows_in):
            return pl.BlockSpec((rows_in, width), lambda g: (0, base + g))

        three = pl.BlockSpec((blocks, NS, width), lambda g: (0, 0, base + g))
        wide = half * width
        return call(
            partial(back_kernel, blocks, heads, base), (half,),
            [SMEM, whole((tokens, NS)), lane_rows, lane_rows, whole((model, ext_rows)), at(TABLE),
             at(ext_rows), at(tokens), at(tokens), whole((tokens, NS)), lane_rows, lane_rows,
             three, at(sent_rows), at(sent_rows), three, at(2 * blocks)],
            [((half // 2, model, width), BF16, pair_of(model, width)),
             ((half // 2, model, width), BF16, pair_of(model, width)),
             ((ext_rows, wide), BF16, cols_of(ext_rows, width)),
             ((tokens, NS), F32, whole((tokens, NS))),
             ((tokens, LANES), F32, lane_rows),
             ((tokens, LANES), F32, lane_rows),
             ((8, wide), F32, cols_of(8, width)),
             ((8, wide), F32, cols_of(8, width))],
            [pltpu.VMEM((ext_rows, width), F32)], "back", 11,
            flags, *sums_in, nx_t, table, x_pre, dy, du, b16, dtp, cump, hloc, before, after, dst,
            fade, after=waits,
        )

    zero = jnp.zeros((tokens, LANES), F32)
    keep1, give1, d_xpre1, *sums1, fdh1, dtaps1 = run_back(0, (zero, zero, zero), (dn_z,))
    state2 = run2.send(state2)
    keep3, give3, d_xpre3, *sums3, fdh3, dtaps3 = run_back(half, sums1, state2)
    db, q, gdt = sums3
    fdh = jnp.concatenate([fdh1, fdh3], axis=1)
    dtaps = jnp.concatenate([dtaps1, dtaps3], axis=1)
    run1 = reduce_shards([(keep1, give1), (keep3, give3)])
    state2 = run2.send(state2)
    tall = pl.BlockSpec((members // 2, tile, width), lambda n: (0, n, 0))
    half_rows = whole((ext_rows, half * width))
    state1 = next(run1)
    (dn_x,) = call(
        partial(norm_back_kernel, blocks), (4,),
        [SMEM, tall, tall, half_rows, half_rows, cols_of(tokens, tile)],
        [((ext_rows, model), F32, cols_of(ext_rows, tile))],
        [], "norm_back", 6, flags, wx_own, wx_other, d_xpre1, d_xpre3, dn_z,
        after=state2 + state1,
    )
    stays1, stays2, mine2, dn_x = lax.optimization_barrier(
        (state1[0], state1[2], state2[0], dn_x)
    )
    state2 = (mine2,) + state2[1:]
    state1 = run1.send((stays1, state1[1], stays2, state1[3]))
    bd = 2 * NS + LANES
    ins = [nx, wbd, taps_bc, bias_bc, rate, bc_pre, dbc, dc, db, raw, step, rows, cols, row, q,
           gdt, fdh, dn_x, x_ext, rstd]
    dw_bd, d_norm, gain_part, dtaps_bc, ddt = call(
        partial(last_kernel, blocks, heads), (1,),
        [SMEM] + [whole(v.shape) for v in ins],
        [((bd, model), BF16, whole((bd, model))),
         ((ext_rows, model), F32, whole((ext_rows, model))),
         ((1, model), F32, whole((1, model))),
         ((8, 2 * NS), F32, whole((8, 2 * NS))),
         ((8, LANES), F32, whole((8, LANES)))],
        [pltpu.VMEM((ext_rows, bd), F32)], "last", 9, flags, *ins, after=state1,
    )

    stays1, stays2, d_norm = lax.optimization_barrier((state1[0], state1[2], d_norm))
    state1 = (stays1, state1[1], stays2, state1[3])

    d_skip_all = sums[1].reshape(members, group_heads, HEAD).sum(axis=2)

    def by_member(v, wide):
        return v.reshape(v.shape[0], members, wide).transpose(1, 0, 2).reshape(members, -1)

    small_grads = jnp.concatenate(
        [by_member(dtaps[:CONV], width), by_member(dtaps[CONV : CONV + 1], width),
         by_member(sums[0:1], width), by_member(dtaps_bc[:CONV], bc_cols),
         by_member(dtaps_bc[CONV : CONV + 1], bc_cols),
         ddt[0, :heads].reshape(members, -1), ddt[1, :heads].reshape(members, -1), d_skip_all],
        axis=1,
    )
    small_grads = jnp.pad(
        small_grads, ((0, 0), (0, small_rows * model - small_grads.shape[1]))
    ).reshape(members, small_rows, model)
    extra = jnp.concatenate(
        [dw_bd[: 2 * NS].reshape(members, bc_cols, model),
         dw_bd[2 * NS : 2 * NS + heads].reshape(members, group_heads, model),
         small_grads.astype(BF16),
         jnp.broadcast_to(gain_part[None], (members, 1, model)).astype(BF16)], axis=1,
    )
    extra = jnp.pad(extra, ((0, 0), (0, -extra.shape[1] % 16), (0, 0)))
    run3 = reduce_small(extra.reshape(members // 2, 2, -1, model))
    states = in_step([run1, run2, run3], [state1, state2, None])
    g1, g2, g3 = (jnp.concatenate(v, axis=0).astype(F32) for v in states)

    from_next = lax.ppermute(d_norm[:HALO], RC, back)
    d_normed = d_norm[HALO:]
    d_normed = jnp.concatenate(
        [d_normed[: tokens - HALO], d_normed[tokens - HALO :] + from_next], axis=0
    )
    x_rows = block_input.astype(F32)
    r_own = rstd[HALO:]
    d_v = d_normed * gain_in
    d_x = (
        d_out.astype(F32) + r_own * d_v
        - x_rows * r_own**3 * jnp.mean(d_v * x_rows, axis=1, keepdims=True)
    )
    flat = g3[side : side + small_rows].reshape(-1)
    s = [flat[cuts[i] : cuts[i + 1]] for i in range(len(sizes))]
    return (
        block_out,
        d_x,
        g3[side + small_rows],
        g2[:width].T,
        g1,
        g3[:bc_cols].T,
        g3[bc_cols:side].T,
        s[0].reshape(CONV, width),
        s[1],
        s[3].reshape(CONV, bc_cols),
        s[4],
        s[5],
        s[6],
        s[7],
        s[2],
        g2[width:],
    )


def solution(mesh):
    placed = (
        P(("dp", "row", "col"), None),
        P(("dp", "row", "col"), None),
        P("dp", None),
        P(),
        P(None, ("row", "col")),
        P(None, ("row", "col")),
        P(None, ("row", "col")),
        P(None, ("row", "col")),
        P(None, ("row", "col")),
        P(("row", "col")),
        P(None, ("row", "col")),
        P(("row", "col")),
        P(("row", "col")),
        P(("row", "col")),
        P(("row", "col")),
        P(("row", "col")),
        P(("row", "col"), None),
    )
    return jax.shard_map(
        on_device,
        mesh=mesh,
        in_specs=placed,
        out_specs=(
            P(("dp", "row", "col"), None),
            P(("dp", "row", "col"), None),
            P(),
            P(None, ("row", "col")),
            P(None, ("row", "col")),
            P(None, ("row", "col")),
            P(None, ("row", "col")),
            P(None, ("row", "col")),
            P(("row", "col")),
            P(None, ("row", "col")),
            P(("row", "col")),
            P(("row", "col")),
            P(("row", "col")),
            P(("row", "col")),
            P(("row", "col")),
            P(("row", "col"), None),
        ),
        check_vma=False,
    )
```

```python
from functools import partial

import jax
import jax.numpy as jnp
from jax import lax
from jax.experimental import pallas as pl
from jax.experimental.pallas import tpu as pltpu
from jax.sharding import PartitionSpec as P

HEAD = 64
NS = 128
CONV = 4
BLOCK = 256
LONGEST = 2048
HALO = 16
LANES = 128
EPS = 1e-05
F32 = jnp.float32
BF16 = jnp.bfloat16
HIGHEST = lax.Precision.HIGHEST
RC = ("row", "col")
NT = (((1,), (1,)), ((), ()))
TN = (((0,), (0,)), ((), ()))
VMEM_LIMIT = 56 * 1024 * 1024
BIAS, GAIN, SKIP, TABLE = 4, 5, 6, 8


def dot(a, b, dims=(((1,), (0,)), ((), ()))):
    return lax.dot_general(a, b, dims, preferred_element_type=F32)


def split3(v, lane, heads):
    hi = v.astype(BF16)
    left = v - hi.astype(F32)
    mid = left.astype(BF16)
    lo = (left - mid.astype(F32)).astype(BF16)
    hi, mid, lo = (p.astype(F32) for p in (hi, mid, lo))
    return jnp.where(lane < heads, hi, jnp.where(lane < 2 * heads, mid, lo)).astype(BF16)


def spread(first, width, heads):
    lane = lax.broadcasted_iota(jnp.int32, (LANES, width), 0)
    head = first + lax.broadcasted_iota(jnp.int32, (LANES, width), 1) // HEAD
    hit = (lane == head) | (lane == head + heads) | (lane == head + 2 * heads)
    return jnp.where(hit, 1.0, 0.0).astype(BF16)


def gather_heads(first, width):
    head = first + lax.broadcasted_iota(jnp.int32, (width, LANES), 0) // HEAD
    lane = lax.broadcasted_iota(jnp.int32, (width, LANES), 1)
    return jnp.where(head == lane, 1.0, 0.0).astype(BF16)


def head_sum(v, to_lanes):
    return dot(v.astype(BF16), to_lanes)


def shifted(ext, block, keep):
    start = HALO - 8 + block * BLOCK
    slab = ext[start : start + BLOCK + 8]
    row = lax.broadcasted_iota(jnp.int32, slab.shape, 0)
    slab = jnp.where(row < 8, slab * keep, slab)
    return [slab[8:]] + [pltpu.roll(slab, o, 0)[8:] for o in range(1, CONV)]


def conv_rows(parts, taps, bias):
    total = parts[0] * taps[CONV - 1 : CONV] + bias
    for o in range(1, CONV):
        total = total + parts[o] * taps[CONV - 1 - o : CONV - o]
    return total


def sigmoid(v):
    return 1.0 / (1.0 + jnp.exp(-v))


def conv_back(d_sum, taps):
    zero = jnp.zeros((8, d_sum.shape[1]), F32)
    slab = jnp.concatenate([zero, d_sum, zero], axis=0)
    rows = slab.shape[0]
    total = slab * taps[CONV - 1 : CONV]
    for o in range(1, CONV):
        total = total + pltpu.roll(slab, rows - o, 0) * taps[CONV - 1 - o : CONV - o]
    return total[: BLOCK + 8]


def prep_kernel(
    blocks, heads,
    flags, nx, wbd, taps, bias, dt_bias, rate,
    bc_pre_o, b_o, c_o, bt_o, ct_o, raw_o, dt_o, dtp_o, cum_o, cump_o, cumt_o,
):
    pre = dot(nx[...], wbd[...], NT).astype(BF16)
    bc_pre_o[...] = pre[:, : 2 * NS]
    ext = pre[:, : 2 * NS].astype(F32)
    raw = pre[HALO:, 2 * NS :].astype(F32) + dt_bias[...]
    raw_o[...] = raw
    step = jnp.maximum(raw, 0.0) + jnp.log1p(jnp.exp(-jnp.abs(raw)))
    lane = lax.broadcasted_iota(jnp.int32, step.shape, 1)
    dt_o[...] = step
    dtp_o[...] = split3(jnp.where(lane < 3 * heads, step, 0.0), lane, heads)
    scaled = step * rate[...]
    tri = jnp.where(
        lax.broadcasted_iota(jnp.int32, (BLOCK, BLOCK), 0)
        >= lax.broadcasted_iota(jnp.int32, (BLOCK, BLOCK), 1),
        1.0,
        0.0,
    )
    for b in range(blocks):
        at = slice(b * BLOCK, (b + 1) * BLOCK)
        cum = jnp.dot(tri, scaled[at], precision=HIGHEST, preferred_element_type=F32)
        cum_o[at, :] = cum
        cump_o[at, :] = split3(cum, lane[at], heads)
        cumt_o[:, at] = cum.T
        conv = conv_rows(shifted(ext, b, flags[b]), taps[...], bias[...])
        bc = (conv * sigmoid(conv)).astype(BF16)
        b_o[at, :] = bc[:, :NS]
        c_o[at, :] = bc[:, NS:]
        bc32 = bc.astype(F32)
        bt_o[:, at] = bc32[:, :NS].T.astype(BF16)
        ct_o[:, at] = bc32[:, NS:].T.astype(BF16)


def state_kernel(
    blocks, heads,
    flags, nx, w, w_other, table, dtp, cump, bt,
    pre_o, x_o, hloc_o, sent_o, fade_o,
):
    g = pl.program_id(0)
    width = x_o.shape[1]
    own = g % 2 == flags[2 * blocks].astype(jnp.int32)
    pre = dot(nx[...], jnp.where(own, w[0], w_other[0])).astype(BF16)
    pre_o[...] = pre
    ext = pre.astype(F32)
    to_cols = spread(g * (width // HEAD), width, heads)
    dt = dot(dtp[...], to_cols)
    cum = dot(cump[...], to_cols)
    carried = jnp.zeros((NS, width), F32)
    through = jnp.ones((1, width), F32)
    for b in range(blocks):
        at = slice(b * BLOCK, (b + 1) * BLOCK)
        conv = conv_rows(shifted(ext, b, flags[b]), table[:CONV], table[BIAS : BIAS + 1])
        x = conv * sigmoid(conv)
        x_o[at, :] = x.astype(BF16)
        cum_b = cum[at]
        last = cum_b[BLOCK - 1 : BLOCK]
        tail = (x * dt[at] * jnp.exp(last - cum_b)).astype(BF16)
        fade = jnp.exp(last)
        carried = carried * flags[b]
        through = through * flags[b]
        hloc_o[b] = carried.astype(BF16)
        fade_o[b : b + 1, :] = through
        fade_o[blocks + b : blocks + b + 1, :] = fade
        carried = fade * carried + dot(bt[:, at], tail)
        through = through * fade
    sent_o[:NS, :] = carried.astype(BF16)
    sent_o[NS:, :] = jnp.broadcast_to(through, (sent_o.shape[0] - NS, width)).astype(BF16)


def head_column(cum, head):
    lane = lax.broadcasted_iota(jnp.int32, cum.shape, 1)
    return jnp.sum(jnp.where(lane == head, cum, 0.0), axis=1, keepdims=True)


def stacked(v, count):
    head = lax.broadcasted_iota(jnp.int32, v.shape, 1) // HEAD
    return jnp.concatenate(
        [jnp.where(head == i, v, 0.0).astype(BF16) for i in range(count)], axis=0
    )


def inner_kernel(blocks, heads, table, b_in, c_in, x_in, dtp, cum_in, cumt_in, y_o, scores):
    g = pl.program_id(0)
    width = y_o.shape[1]
    count = width // HEAD

    @pl.when(g == 0)
    def _():
        for b in range(blocks):
            at = slice(b * BLOCK, (b + 1) * BLOCK)
            scores[b] = dot(c_in[at, :], b_in[at, :], NT)

    dt = dot(dtp[...], spread(g * count, width, heads))
    lower = lax.broadcasted_iota(jnp.int32, (BLOCK, BLOCK), 0) >= lax.broadcasted_iota(
        jnp.int32, (BLOCK, BLOCK), 1
    )
    for b in range(blocks):
        at = slice(b * BLOCK, (b + 1) * BLOCK)
        x = x_in[at, :].astype(F32)
        u = stacked(x * dt[at], count)
        cum = cum_in[at, :]
        weights = []
        for i in range(count):
            h = g * count + i
            diff = head_column(cum, h) - cumt_in[pl.ds(h, 1), at]
            decay = jnp.exp(jnp.where(lower, diff, -1e30))
            weights.append((scores[b] * decay).astype(BF16))
        y = dot(jnp.concatenate(weights, axis=1), u)
        y_o[at, :] = (y + x * table[SKIP : SKIP + 1]).astype(BF16)


def project_kernel(nx, d_mix, w, z_o, back_o):
    width = z_o.shape[1]
    z_o[...] = dot(nx[HALO:, :], w[0, :width], NT).astype(BF16)
    back_o[...] = dot(d_mix[...], w[0, width:], NT).astype(BF16)


def middle_kernel(
    heads,
    table, y_in, z_in, x_in, back_in, c_in, ct_in, cump, hloc, before, fade,
    yout_o, dy_o, dz_o, row_o, dc_o, dst_o, sums_o, sent_o,
):
    b = pl.program_id(0)
    width = y_in.shape[1]
    through = fade[pl.ds(b, 1), :]
    enter = (through * before[:NS].astype(F32) + hloc[0].astype(F32)).astype(BF16)
    grow = jnp.exp(dot(cump[...], spread(0, width, heads)))
    across = dot(c_in[...], enter) * grow
    y = y_in[...].astype(F32) + across
    z = z_in[...].astype(F32)
    gate = sigmoid(z)
    silu = z * gate
    gated = y * silu
    rs = lax.rsqrt(jnp.sum(gated * gated, axis=1, keepdims=True) / width + EPS)
    unit = gated * rs
    gain = table[GAIN : GAIN + 1]
    yout_o[...] = (unit * gain).astype(BF16)
    back = back_in[...].astype(F32)
    d_unit = back * gain
    along = jnp.sum(d_unit * gated, axis=1, keepdims=True) / width
    d_gated = rs * d_unit - gated * (rs * rs * rs * along)
    dy = d_gated * silu
    dy_o[...] = dy.astype(BF16)
    dz_o[...] = (d_gated * y * (gate * (1.0 + z * (1.0 - gate)))).astype(BF16)
    row_o[...] = head_sum(dy * across, gather_heads(0, width))
    grown = (dy * grow).astype(BF16)
    dc_o[...] = dot(grown, enter, NT)
    dst = dot(ct_in[...], grown)
    dst_o[0] = dst.astype(BF16)

    @pl.when(b == 0)
    def _():
        sums_o[...] = jnp.zeros_like(sums_o)
        sent_o[...] = jnp.zeros_like(sent_o)

    sums_o[0:1] += jnp.sum(back * unit, axis=0, keepdims=True)
    sums_o[1:2] += jnp.sum(dy * x_in[...].astype(F32), axis=0, keepdims=True)
    sent_o[...] += through * dst


def weights_kernel(blocks, flags, nx, d_mix, dz, yout, keep_o, give_o):
    g = pl.program_id(0)
    width = dz.shape[1]
    own = g % 2 == flags[2 * blocks].astype(jnp.int32)
    dw_z = dot(dz[...], nx[HALO:, :], TN).astype(BF16)
    dw_out = dot(yout[...], d_mix[...], TN).astype(BF16)

    @pl.when(own)
    def _():
        keep_o[0, :width] = dw_z
        keep_o[0, width:] = dw_out

    @pl.when(jnp.logical_not(own))
    def _():
        give_o[0, :width] = dw_z
        give_o[0, width:] = dw_out


def mix_kernel(blocks, flags, w, dz, yout, x_rows, dn_o, out_o):
    inner = dz.shape[1]
    width = inner // w.shape[0]
    tile = out_o.shape[1]
    dn_o[...] = dot(dz[...], w[:, :width, :].reshape(inner, tile))
    mix = dot(yout[...], w[:, width:, :].reshape(inner, tile))
    for b in range(blocks):
        at = slice(b * BLOCK, (b + 1) * BLOCK)
        live = flags[blocks + b]
        out_o[at, :] = (x_rows[at, :].astype(F32) + live * mix[at]).astype(BF16)


def norm_back_kernel(blocks, flags, w, w_other, d_pre_a, d_pre_b, dn_z, dn_o):
    first = flags[2 * blocks] == 0.0
    members = []
    for z in range(w.shape[0]):
        members += [jnp.where(first, w[z], w_other[z]), jnp.where(first, w_other[z], w[z])]
    half = len(members) // 2
    total = dot(d_pre_a[...], jnp.concatenate(members[:half], axis=1), NT)
    total += dot(d_pre_b[...], jnp.concatenate(members[half:], axis=1), NT)
    dn_o[:HALO, :] = total[:HALO]
    dn_o[HALO:, :] = total[HALO:] + dn_z[...]


def inner_back_kernel(
    blocks, heads,
    b_in, c_in, x_in, dy_in, dtp, cum_in, cumt_in,
    du_o, dbc_o, rows_o, cols_o, scores, d_scores,
):
    g = pl.program_id(0)
    width = du_o.shape[1]
    count = width // HEAD

    @pl.when(g == 0)
    def _():
        d_scores[...] = jnp.zeros_like(d_scores)
        cols_o[...] = jnp.zeros_like(cols_o)
        for b in range(blocks):
            at = slice(b * BLOCK, (b + 1) * BLOCK)
            scores[b] = dot(b_in[at, :], c_in[at, :], NT)

    rows_o[...] = jnp.zeros_like(rows_o)
    dt = dot(dtp[...], spread(g * count, width, heads))
    lower = lax.broadcasted_iota(jnp.int32, (BLOCK, BLOCK), 0) <= lax.broadcasted_iota(
        jnp.int32, (BLOCK, BLOCK), 1
    )
    for b in range(blocks):
        at = slice(b * BLOCK, (b + 1) * BLOCK)
        u = (x_in[at, :].astype(F32) * dt[at]).astype(BF16)
        dy = stacked(dy_in[at, :].astype(F32), count)
        d_w = dot(u, dy, NT)
        cum = cum_in[at, :]
        lane = lax.broadcasted_iota(jnp.int32, cum.shape, 1)
        cols = cols_o[at, :]
        weights = []
        for i in range(count):
            h = g * count + i
            diff = cumt_in[pl.ds(h, 1), at] - head_column(cum, h)
            decay = jnp.exp(jnp.where(lower, diff, -1e30))
            weights.append((scores[b] * decay).astype(BF16))
            d_score = d_w[:, i * BLOCK : (i + 1) * BLOCK] * decay
            d_scores[b] += d_score
            both = d_score * scores[b]
            rows_o[0, i : i + 1, at] = jnp.sum(both, axis=0, keepdims=True)
            cols = jnp.where(lane == h, jnp.sum(both, axis=1, keepdims=True), cols)
        cols_o[at, :] = cols
        du_o[at, :] = dot(jnp.concatenate(weights, axis=1), dy).astype(BF16)

    @pl.when(g == pl.num_programs(0) - 1)
    def _():
        for b in range(blocks):
            at = slice(b * BLOCK, (b + 1) * BLOCK)
            ds = d_scores[b].astype(BF16)
            dbc_o[at, :NS] = dot(ds, c_in[at, :])
            dbc_o[at, NS:] = dot(ds, b_in[at, :], TN)


def back_kernel(
    blocks, heads, base,
    flags, db_in, q_in, gdt_in, nx_t, table, pre_in, dy_in, du_in, b_in, dtp, cump, hloc, before, after, dst, fade,
    keep_o, give_o, d_pre_o, db_o, q_o, gdt_o, fdh_o, dtap_o, d_ext,
):
    g = pl.program_id(0)
    width = dy_in.shape[1]
    first = (base + g) * (width // HEAD)

    @pl.when(g == 0)
    def _():
        db_o[...] = db_in[...]
        q_o[...] = q_in[...]
        gdt_o[...] = gdt_in[...]

    to_cols = spread(first, width, heads)
    to_lanes = gather_heads(first, width)
    dt_all = dot(dtp[...], to_cols)
    cum_all = dot(cump[...], to_cols)
    ext = pre_in[...].astype(F32)
    taps = table[:CONV]
    skip = table[SKIP : SKIP + 1]
    d_states = [None] * blocks
    d_state = after[:NS].astype(F32)
    for b in reversed(range(blocks)):
        d_states[b] = d_state
        fade_b = fade[blocks + b : blocks + b + 1]
        d_state = flags[b] * (fade_b * d_state + dst[b].astype(F32))
    d_ext[:HALO, :] = jnp.zeros((HALO, width), F32)
    d_taps = [jnp.zeros((1, width), F32) for _ in range(CONV + 1)]
    fdh_o[...] = jnp.zeros_like(fdh_o)
    for b in range(blocks):
        at = slice(b * BLOCK, (b + 1) * BLOCK)
        enter = fade[b : b + 1] * before[:NS].astype(F32) + hloc[b].astype(F32)
        fdh_o[b : b + 1, :] = fade[blocks + b : blocks + b + 1] * jnp.sum(
            enter * d_states[b], axis=0, keepdims=True
        )
        d_st = d_states[b].astype(BF16)
        parts = shifted(ext, b, flags[b])
        conv = conv_rows(parts, taps, table[BIAS : BIAS + 1])
        sig = sigmoid(conv)
        x = conv * sig
        dt = dt_all[at]
        cum = cum_all[at]
        tail = jnp.exp(cum[BLOCK - 1 : BLOCK] - cum)
        u = x * dt
        du_state = dot(b_in[at, :], d_st) * tail
        du = du_in[at, :].astype(F32) + du_state
        db_o[at, :] += dot((u * tail).astype(BF16), d_st, NT)
        q_o[at, :] += head_sum(u * du_state, to_lanes)
        gdt_o[at, :] += head_sum(x * du, to_lanes)
        dx = dt * du + skip * dy_in[at, :].astype(F32)
        d_sum = dx * (sig * (1.0 + conv * (1.0 - sig)))
        for o in range(CONV):
            d_taps[CONV - 1 - o] += jnp.sum(d_sum * parts[o], axis=0, keepdims=True)
        d_taps[CONV] += jnp.sum(d_sum, axis=0, keepdims=True)
        carried = conv_back(d_sum, taps)
        start = HALO + b * BLOCK
        d_ext[start - 8 : start, :] += flags[b] * carried[:8]
        d_ext[start : start + BLOCK, :] = carried[8:]
    dtap_o[...] = jnp.concatenate(d_taps + [jnp.zeros((3, width), F32)], axis=0)
    d_pre = d_ext[...].astype(BF16)
    d_pre_o[...] = d_pre
    dw = dot(nx_t[...], d_pre).astype(BF16)
    own = g % 2 == flags[2 * blocks].astype(jnp.int32)

    @pl.when(own)
    def _():
        keep_o[0] = dw

    @pl.when(jnp.logical_not(own))
    def _():
        give_o[0] = dw


def last_kernel(
    blocks, heads,
    flags, nx, wbd, taps_in, bias, rate, bc_pre, dbc, dc, db, raw, step_in,
    rows, cols, row, q, gdt, fdh, dn_x, x_ext, rstd,
    dw_o, dn_o, gain_o, dtap_o, ddt_o, d_ext,
):
    taps = taps_in[...]
    ext = bc_pre[...].astype(F32)
    width = ext.shape[1]
    d_ext[:HALO, :] = jnp.zeros((HALO, d_ext.shape[1]), F32)
    d_taps = [jnp.zeros((1, width), F32) for _ in range(CONV + 1)]
    bias_sum = jnp.zeros((1, LANES), F32)
    rate_sum = jnp.zeros((1, LANES), F32)
    row_i = lax.broadcasted_iota(jnp.int32, (BLOCK, BLOCK), 0)
    col_i = lax.broadcasted_iota(jnp.int32, (BLOCK, BLOCK), 1)
    onward = jnp.where(row_i <= col_i, 1.0, 0.0)
    earlier = jnp.where(row_i > col_i, 1.0, 0.0)
    lane = lax.broadcasted_iota(jnp.int32, (BLOCK, LANES), 1)
    faded = jnp.dot(
        fdh[...], gather_heads(0, fdh.shape[1]).astype(F32), precision=HIGHEST,
        preferred_element_type=F32,
    )
    for b in range(blocks):
        at = slice(b * BLOCK, (b + 1) * BLOCK)
        start = HALO + b * BLOCK
        flow = rows[at, :] - cols[at, :] + row[at, :]
        d_a = (
            jnp.dot(onward, flow, precision=HIGHEST, preferred_element_type=F32)
            + jnp.dot(earlier, q[at, :], precision=HIGHEST, preferred_element_type=F32)
            + faded[b : b + 1]
        )
        step = step_in[at, :]
        d_step = gdt[at, :] + rate[...] * d_a
        d_raw = jnp.where(lane < heads, d_step * sigmoid(raw[at, :]), 0.0)
        bias_sum += jnp.sum(d_raw, axis=0, keepdims=True)
        rate_sum += jnp.sum(step * d_a, axis=0, keepdims=True)
        d_ext[start : start + BLOCK, 2 * NS :] = d_raw
        parts = shifted(ext, b, flags[b])
        conv = conv_rows(parts, taps, bias[...])
        sig = sigmoid(conv)
        d_bc = dbc[at, :] + jnp.concatenate([db[at, :], dc[at, :]], axis=1)
        d_sum = d_bc * (sig * (1.0 + conv * (1.0 - sig)))
        for o in range(CONV):
            d_taps[CONV - 1 - o] += jnp.sum(d_sum * parts[o], axis=0, keepdims=True)
        d_taps[CONV] += jnp.sum(d_sum, axis=0, keepdims=True)
        carried = conv_back(d_sum, taps)
        d_ext[start - 8 : start, : 2 * NS] += flags[b] * carried[:8]
        d_ext[start : start + BLOCK, : 2 * NS] = carried[8:]
    dtap_o[...] = jnp.concatenate(d_taps + [jnp.zeros((3, width), F32)], axis=0)
    ddt_o[...] = jnp.concatenate(
        [bias_sum, rate_sum * rate[...], jnp.zeros((6, LANES), F32)], axis=0
    )
    d_pre = d_ext[...].astype(BF16)
    dw_o[...] = dot(d_pre, nx[...], TN).astype(BF16)
    total = dn_x[...] + dot(d_pre, wbd[...])
    dn_o[...] = total
    gain_o[...] = jnp.sum(total * (x_ext[...].astype(F32) * rstd[...]), axis=0, keepdims=True)


def whole(shape):
    rank = len(shape)
    return pl.BlockSpec(shape, lambda *_: (0,) * rank)


SMEM = pl.BlockSpec(memory_space=pltpu.SMEM)


def cols_of(rows, width):
    return pl.BlockSpec((rows, width), lambda g: (0, g))


def member_of(rows, width):
    return pl.BlockSpec((1, rows, width), lambda g: (g, 0, 0))


def pair_of(rows, width):
    return pl.BlockSpec((1, rows, width), lambda g: (g // 2, 0, 0))


def call(kernel, grid, ins, outs, scratch, name, us, *args, after=()):
    count = len(args)

    def body(*refs):
        kernel(*refs[:count], *refs[count + len(after) :])

    return pl.pallas_call(
        body,
        grid=grid,
        in_specs=list(ins) + [pl.BlockSpec(memory_space=pl.ANY)] * len(after),
        out_specs=[spec for _, _, spec in outs],
        out_shape=[jax.ShapeDtypeStruct(shape, dtype) for shape, dtype, _ in outs],
        scratch_shapes=scratch,
        compiler_params=pltpu.CompilerParams(vmem_limit_bytes=VMEM_LIMIT),
        cost_estimate=pl.CostEstimate(
            flops=int(us * 1.1e9), bytes_accessed=int(us * 1e6), transcendentals=0
        ),
        name=name,
    )(*args, *after)


def state_scan(own, members, tokens, forward, beside=()):
    def moved(v, by):
        pairs = [(i, i + by) for i in range(members - by)]
        if not forward:
            pairs = [(b, a) for a, b in pairs]
        return lax.ppermute(v, RC, pairs)

    reach = min(members - 1, -(-LONGEST // tokens))
    is_term = lax.broadcasted_iota(jnp.int32, own.shape, 0) < NS
    steps = []
    span = 1
    while span < reach:
        got = moved(own, span).astype(F32)
        if len(steps) < len(beside):
            own, _ = lax.optimization_barrier((own, beside[len(steps)]))
        held = own.astype(F32)
        own = (jnp.where(is_term, held, 0.0) + held[NS : NS + 1] * got).astype(BF16)
        steps.append(own)
        span *= 2
    steps.append(moved(own, 1))
    return steps


def thrice(v):
    hi = lax.optimization_barrier(v.astype(BF16))
    left = v - hi.astype(F32)
    mid = lax.optimization_barrier(left.astype(BF16))
    lo = (left - mid.astype(F32)).astype(BF16)
    return jnp.stack([hi, mid, lo])


def halves(v, axis):
    half = v.shape[axis] // 2
    return lax.slice_in_dim(v, 0, half, axis=axis), lax.slice_in_dim(v, half, None, axis=axis)


def dp_bits():
    return [1 << i for i in range((lax.axis_size("dp") - 1).bit_length())]


def across_dp(v, bit):
    return lax.ppermute(v, "dp", [(i, i ^ bit) for i in range(lax.axis_size("dp"))])


def set_bit(bit):
    return (lax.axis_index("dp") // bit) % 2 == 1


def gather_dp(v, axis):
    bits = dp_bits()
    me = lax.axis_index("dp")
    for low in range(0, len(bits), 2):
        count = 1 << len(bits[low : low + 2])
        mine = (me // bits[low]) % count
        size = v.shape[axis]
        shape = list(v.shape)
        shape[axis] = size * count
        out = jnp.zeros(shape, v.dtype)
        for by in range(count):
            piece = across_dp(v, by * bits[low]) if by else v
            out = lax.dynamic_update_slice_in_dim(out, piece, (mine ^ by) * size, axis)
        v = out
    return v


def double(v, bit, axis):
    got = across_dp(v, bit)
    up = set_bit(bit)
    return jnp.concatenate([jnp.where(up, got, v), jnp.where(up, v, got)], axis=axis)


def doubled(v, bits, axis):
    for bit in bits:
        v = double(v, bit, axis)
    return v


def to_halve(v, bit, axis):
    low, high = halves(v, axis)
    up = set_bit(bit)
    return jnp.where(up, high, low), jnp.where(up, low, high)


def summed(stays, goes, bit):
    return (stays.astype(F32) + across_dp(goes, bit).astype(F32)).astype(BF16)


def along_row(v, by):
    rows = lax.axis_size("row")
    return lax.ppermute(v, "row", [(i, (i + by) % rows) for i in range(rows)])


def other_col(v):
    return lax.ppermute(v, "col", [(0, 1), (1, 0)])


def gather_rows(v):
    rows = lax.axis_size("row")
    row = lax.axis_index("row")
    out = jnp.zeros((rows,) + v.shape, v.dtype)
    for by in range(rows):
        piece = v if by == 0 else along_row(v, by)
        out = lax.dynamic_update_index_in_dim(out, piece, (row - by) % rows, 0)
    return out


def row_pieces(v):
    rows = lax.axis_size("row")
    row = lax.axis_index("row")
    return tuple(
        lax.dynamic_index_in_dim(v, (row + by) % rows, 0, keepdims=False) for by in range(rows)
    )


def sum_rows(pieces):
    terms = [(p if by == 0 else along_row(p, by)).astype(F32) for by, p in enumerate(pieces)]
    while len(terms) > 1:
        half = len(terms) // 2
        terms = [terms[i] + terms[i + half] for i in range(half)]
    return terms[0]


def reduce_shards(parts):
    bits = dp_bits()
    sums = [(k.astype(F32) + other_col(v).astype(F32)).astype(BF16) for k, v in parts]
    now = halves(jnp.concatenate(sums, axis=0), 1)
    for one, two in zip(bits[::-1], bits):
        a, b, c, d = yield to_halve(now[0], one, 1) + to_halve(now[1], two, 1)
        now = summed(a, b, one), summed(c, d, two)
    cut = now[0].shape[1]
    pieces = yield row_pieces(jnp.concatenate(now, axis=1))
    (part,) = yield (sum_rows(pieces).astype(BF16),)
    n = lax.axis_size("dp")
    whole_sum = gather_dp(part[None], 0)
    first = whole_sum[:, :cut]
    second = whole_sum[:, cut:]
    count = len(bits)
    shape = second.shape
    second = second.reshape((2,) * count + shape[1:])
    second = second.transpose(tuple(reversed(range(count))) + (count, count + 1)).reshape(shape)
    yield (first.reshape(n * cut, -1), second.reshape(n * cut, -1))


def reduce_small(v):
    even, odd = v[:, 0], v[:, 1]
    first = lax.axis_index("col") == 0
    both = jnp.where(first, even, odd).astype(F32) + other_col(
        jnp.where(first, odd, even)
    ).astype(F32)
    pieces = yield row_pieces(both.astype(BF16))
    now = yield (sum_rows(pieces),)
    for bit in dp_bits():
        now = yield (now[0] + across_dp(now[0], bit),)


def in_step(runs, states):
    running = list(range(len(runs)))
    while running:
        left = []
        for i in running:
            try:
                states[i] = next(runs[i]) if states[i] is None else runs[i].send(states[i])
                left.append(i)
            except StopIteration:
                pass
        running = left
        if running:
            tied = lax.optimization_barrier([states[i] for i in running])
            for i, value in zip(running, tied):
                states[i] = value
    return states


def gather_shards(v):
    bits = dp_bits()
    me = lax.axis_index("dp")
    turned = sum(((me // bit) % 2) * back for bit, back in zip(bits, bits[::-1]))
    first, second = halves(v, 0)
    rows = first.shape[0] // lax.axis_size("dp")
    mine = jnp.concatenate(
        [lax.dynamic_slice_in_dim(first, me * rows, rows, 0),
         lax.dynamic_slice_in_dim(second, turned * rows, rows, 0)], axis=0
    )
    got = gather_rows(mine)
    first = doubled(got[:, :rows], bits, 1)
    second = doubled(got[:, rows:], bits[::-1], 1)
    own = jnp.concatenate([first, second], axis=1)
    return own, other_col(own)


def on_device(
    block_input, d_out, lengths, gain_in, w_z, w_x, w_bc, w_dt, conv_x, conv_x_bias,
    conv_bc, conv_bc_bias, dt_bias, a_log, d_skip, gain_gate, w_out,
):
    members = lax.axis_size(RC)
    place = lax.axis_index(RC)
    tokens, model = block_input.shape
    blocks = tokens // BLOCK
    width = w_x.shape[1]
    inner = width * members
    group_heads = w_dt.shape[1]
    heads = group_heads * members
    bc_cols = w_bc.shape[1]
    ext_rows = tokens + HALO

    small = jnp.concatenate(
        [conv_x.reshape(-1), conv_x_bias, gain_gate, conv_bc.reshape(-1), conv_bc_bias,
         dt_bias, a_log, d_skip]
    )
    small_rows = -(-small.shape[0] // model)
    parts = thrice(jnp.pad(small, (0, small_rows * model - small.shape[0])))
    side = bc_cols + group_heads
    rows1 = side + 3 * small_rows
    pack1 = jnp.concatenate(
        [w_bc.T, w_dt.T, parts.reshape(3 * small_rows, model),
         jnp.zeros((-rows1 % 16, model), BF16)], axis=0
    )
    col = lax.axis_index("col")
    own1 = gather_rows(pack1)
    other1 = other_col(own1)
    all1 = jnp.where(
        col == 0, jnp.stack([own1, other1], axis=1), jnp.stack([other1, own1], axis=1)
    ).reshape(members, -1, model)
    wx_own, wx_other = gather_shards(w_x)
    pack2 = jnp.concatenate([w_z.T, w_out], axis=0)
    all2 = lax.all_gather(pack2, RC, axis=0)

    ends = jnp.cumsum(lengths[0])
    firsts = jnp.arange(members * blocks, dtype=jnp.int32) * BLOCK

    def segment(at):
        return jnp.sum((at[:, None] >= ends[None, :]).astype(jnp.int32), axis=1)

    kept = (segment(firsts) == segment(firsts - 1)) & (firsts > 0)
    both = jnp.stack([kept, firsts < ends[-1]]).astype(F32)
    flags = lax.dynamic_slice(both, (0, place * blocks), (2, blocks)).reshape(-1)
    flags = jnp.concatenate([flags, col.astype(F32)[None]])

    ahead = [(i, i + 1) for i in range(members - 1)]
    back = [(i + 1, i) for i in range(members - 1)]
    tail_rows = lax.ppermute(block_input[tokens - HALO :], RC, ahead)
    x_ext = jnp.concatenate([tail_rows, block_input], axis=0)
    x32 = x_ext.astype(F32)
    rstd = lax.rsqrt(jnp.mean(x32 * x32, axis=1, keepdims=True) + EPS)
    nx = (x32 * rstd * gain_in).astype(BF16)
    nx_t = nx.T
    live = jnp.repeat(flags[blocks : 2 * blocks], BLOCK)[:, None]
    d_mix = (d_out.astype(F32) * live).astype(BF16)

    w_bc_t = all1[:, :bc_cols].reshape(-1, model)
    w_dt_t = all1[:, bc_cols:side].reshape(-1, model)
    wbd = jnp.concatenate(
        [w_bc_t, w_dt_t, w_dt_t, w_dt_t, jnp.zeros((LANES - 3 * heads, model), BF16)], axis=0
    )
    pieces = all1[:, side : side + 3 * small_rows].astype(F32)
    pieces = pieces.reshape(members, 3, small_rows * model)
    small_all = pieces[:, 0] + pieces[:, 1] + pieces[:, 2]
    sizes = [conv_x.size, width, width, conv_bc.size, bc_cols, group_heads, group_heads, group_heads]
    cuts = [sum(sizes[:i]) for i in range(len(sizes) + 1)]
    s_conv, s_bias, s_gain, s_cbc, s_cbias, s_dtb, s_alog, s_skip = (
        small_all[:, cuts[i] : cuts[i + 1]] for i in range(len(sizes))
    )
    skip_cols = jnp.repeat(s_skip.reshape(-1), HEAD)[None]
    table = jnp.concatenate(
        [s_conv.reshape(members, CONV, width).transpose(1, 0, 2).reshape(CONV, inner),
         s_bias.reshape(1, inner), s_gain.reshape(1, inner), skip_cols,
         jnp.zeros((1, inner), F32)], axis=0
    )
    taps_bc = s_cbc.reshape(members, CONV, bc_cols).transpose(1, 0, 2).reshape(CONV, 2 * NS)
    bias_bc = s_cbias.reshape(1, 2 * NS)

    def lanes(v):
        return jnp.pad(jnp.tile(v.reshape(1, heads), (1, 3)), ((0, 0), (0, LANES - 3 * heads)))

    dtb = lanes(s_dtb)
    rate = lanes(-jnp.exp(s_alog))

    (bc_pre, b16, c16, bt, ct, raw, step, dtp, cum, cump, cumt) = call(
        partial(prep_kernel, blocks, heads), (1,),
        [SMEM, whole((ext_rows, model)), whole(wbd.shape), whole(taps_bc.shape),
         whole(bias_bc.shape), whole((1, LANES)), whole((1, LANES))],
        [((ext_rows, 2 * NS), BF16, whole((ext_rows, 2 * NS))),
         ((tokens, NS), BF16, whole((tokens, NS))),
         ((tokens, NS), BF16, whole((tokens, NS))),
         ((NS, tokens), BF16, whole((NS, tokens))),
         ((NS, tokens), BF16, whole((NS, tokens))),
         ((tokens, LANES), F32, whole((tokens, LANES))),
         ((tokens, LANES), F32, whole((tokens, LANES))),
         ((tokens, LANES), BF16, whole((tokens, LANES))),
         ((tokens, LANES), F32, whole((tokens, LANES))),
         ((tokens, LANES), BF16, whole((tokens, LANES))),
         ((LANES, tokens), F32, whole((LANES, tokens)))],
        [], "prep", 4, flags, nx, wbd, taps_bc, bias_bc, dtb, rate,
    )
    lane_rows = whole((tokens, LANES))
    sent_rows = NS + 16
    x_pre, x16, hloc, own, fade = call(
        partial(state_kernel, blocks, heads), (members,),
        [SMEM, whole((ext_rows, model)), pair_of(model, width), pair_of(model, width),
         cols_of(TABLE, width), lane_rows, lane_rows, whole((NS, tokens))],
        [((ext_rows, inner), BF16, cols_of(ext_rows, width)),
         ((tokens, inner), BF16, cols_of(tokens, width)),
         ((blocks, NS, inner), BF16, pl.BlockSpec((blocks, NS, width), lambda g: (0, 0, g))),
         ((sent_rows, inner), BF16, cols_of(sent_rows, width)),
         ((2 * blocks, inner), F32, cols_of(2 * blocks, width))],
        [], "states", 12, flags, nx, wx_own, wx_other, table, dtp, cump, bt,
    )
    before = state_scan(own, members, tokens, True)[-1]
    (y_loc,) = call(
        partial(inner_kernel, blocks, heads), (members,),
        [cols_of(TABLE, width), whole((tokens, NS)), whole((tokens, NS)), cols_of(tokens, width),
         lane_rows, lane_rows, whole((LANES, tokens))],
        [((tokens, inner), BF16, cols_of(tokens, width))],
        [pltpu.VMEM((blocks, BLOCK, BLOCK), F32)], "inner", 9,
        table, b16, c16, x16, dtp, cum, cumt,
    )
    z_pre, d_yout = call(
        project_kernel, (members,),
        [whole((ext_rows, model)), whole((tokens, model)), member_of(2 * width, model)],
        [((tokens, inner), BF16, cols_of(tokens, width))] * 2,
        [], "project", 11, nx, d_mix, all2,
    )

    def rows_of(cols):
        return pl.BlockSpec((BLOCK, cols), lambda b: (b, 0))

    y_out, dy, dz, row, dc, dst, sums, grad_own = call(
        partial(middle_kernel, heads), (blocks,),
        [whole((TABLE, inner)), rows_of(inner), rows_of(inner), rows_of(inner), rows_of(inner),
         rows_of(NS), pl.BlockSpec((NS, BLOCK), lambda b: (0, b)), rows_of(LANES),
         pl.BlockSpec((1, NS, inner), lambda b: (b, 0, 0)), whole((sent_rows, inner)),
         whole((2 * blocks, inner))],
        [((tokens, inner), BF16, rows_of(inner)),
         ((tokens, inner), BF16, rows_of(inner)),
         ((tokens, inner), BF16, rows_of(inner)),
         ((tokens, LANES), F32, rows_of(LANES)),
         ((tokens, NS), F32, rows_of(NS)),
         ((blocks, NS, inner), BF16, pl.BlockSpec((1, NS, inner), lambda b: (b, 0, 0))),
         ((8, inner), F32, whole((8, inner))),
         ((NS, inner), F32, whole((NS, inner)))],
        [], "middle", 14, table, y_loc, z_pre, x16, d_yout, c16, ct, cump, hloc, before, fade,
    )
    (keep2, give2) = call(
        partial(weights_kernel, blocks), (members,),
        [SMEM, whole((ext_rows, model)), whole((tokens, model)),
         cols_of(tokens, width), cols_of(tokens, width)],
        [((members // 2, 2 * width, model), BF16, pair_of(2 * width, model)),
         ((members // 2, 2 * width, model), BF16, pair_of(2 * width, model))],
        [], "weights", 10, flags, nx, d_mix, dz, y_out,
    )
    grad_own = jnp.concatenate([grad_own.astype(BF16), own[NS:]], axis=0)
    scan = state_scan(grad_own, members, tokens, False, (keep2,))
    give2, _ = lax.optimization_barrier((give2, scan[0]))
    run2 = reduce_shards([(keep2, give2)])
    tile = model // 2
    state2 = next(run2)
    du, dbc, rows, cols = call(
        partial(inner_back_kernel, blocks, heads), (members,),
        [whole((tokens, NS)), whole((tokens, NS)), cols_of(tokens, width), cols_of(tokens, width),
         lane_rows, lane_rows, whole((LANES, tokens))],
        [((tokens, inner), BF16, cols_of(tokens, width)),
         ((tokens, 2 * NS), F32, whole((tokens, 2 * NS))),
         ((members, 8, tokens), F32, member_of(8, tokens)),
         ((tokens, LANES), F32, lane_rows)],
        [pltpu.VMEM((blocks, BLOCK, BLOCK), F32), pltpu.VMEM((blocks, BLOCK, BLOCK), F32)],
        "inner_back", 12, b16, c16, x16, dy, dtp, cum, cumt, after=(scan[0], keep2),
    )
    dn_z, block_out = call(
        partial(mix_kernel, blocks), (2,),
        [SMEM, pl.BlockSpec((members, 2 * width, tile), lambda n: (0, 0, n)),
         whole((tokens, inner)), whole((tokens, inner)), cols_of(tokens, tile)],
        [((tokens, model), F32, cols_of(tokens, tile)),
         ((tokens, model), BF16, cols_of(tokens, tile))],
        [], "mix", 9, flags, all2, dz, y_out, block_input, after=(scan[-2], du) + state2,
    )
    after = scan[-1]
    rows = jnp.pad(
        rows[:, :group_heads].reshape(heads, tokens).T, ((0, 0), (0, LANES - heads))
    )
    half = members // 2

    def run_back(base, sums_in, waits):
        def at(rows_in):
            return pl.BlockSpec((rows_in, width), lambda g: (0, base + g))

        three = pl.BlockSpec((blocks, NS, width), lambda g: (0, 0, base + g))
        wide = half * width
        return call(
            partial(back_kernel, blocks, heads, base), (half,),
            [SMEM, whole((tokens, NS)), lane_rows, lane_rows, whole((model, ext_rows)), at(TABLE),
             at(ext_rows), at(tokens), at(tokens), whole((tokens, NS)), lane_rows, lane_rows,
             three, at(sent_rows), at(sent_rows), three, at(2 * blocks)],
            [((half // 2, model, width), BF16, pair_of(model, width)),
             ((half // 2, model, width), BF16, pair_of(model, width)),
             ((ext_rows, wide), BF16, cols_of(ext_rows, width)),
             ((tokens, NS), F32, whole((tokens, NS))),
             ((tokens, LANES), F32, lane_rows),
             ((tokens, LANES), F32, lane_rows),
             ((8, wide), F32, cols_of(8, width)),
             ((8, wide), F32, cols_of(8, width))],
            [pltpu.VMEM((ext_rows, width), F32)], "back", 11,
            flags, *sums_in, nx_t, table, x_pre, dy, du, b16, dtp, cump, hloc, before, after, dst,
            fade, after=waits,
        )

    zero = jnp.zeros((tokens, LANES), F32)
    keep1, give1, d_xpre1, *sums1, fdh1, dtaps1 = run_back(0, (zero, zero, zero), (dn_z,))
    state2 = run2.send(state2)
    keep3, give3, d_xpre3, *sums3, fdh3, dtaps3 = run_back(half, sums1, state2)
    db, q, gdt = sums3
    fdh = jnp.concatenate([fdh1, fdh3], axis=1)
    dtaps = jnp.concatenate([dtaps1, dtaps3], axis=1)
    run1 = reduce_shards([(keep1, give1), (keep3, give3)])
    state2 = run2.send(state2)
    tall = pl.BlockSpec((members // 2, tile, width), lambda n: (0, n, 0))
    half_rows = whole((ext_rows, half * width))
    state1 = next(run1)
    (dn_x,) = call(
        partial(norm_back_kernel, blocks), (2,),
        [SMEM, tall, tall, half_rows, half_rows, cols_of(tokens, tile)],
        [((ext_rows, model), F32, cols_of(ext_rows, tile))],
        [], "norm_back", 6, flags, wx_own, wx_other, d_xpre1, d_xpre3, dn_z,
        after=state2 + state1,
    )
    stays1, stays2, mine2, dn_x = lax.optimization_barrier(
        (state1[0], state1[2], state2[0], dn_x)
    )
    state2 = (mine2,) + state2[1:]
    state1 = run1.send((stays1, state1[1], stays2, state1[3]))
    bd = 2 * NS + LANES
    ins = [nx, wbd, taps_bc, bias_bc, rate, bc_pre, dbc, dc, db, raw, step, rows, cols, row, q,
           gdt, fdh, dn_x, x_ext, rstd]
    dw_bd, d_norm, gain_part, dtaps_bc, ddt = call(
        partial(last_kernel, blocks, heads), (1,),
        [SMEM] + [whole(v.shape) for v in ins],
        [((bd, model), BF16, whole((bd, model))),
         ((ext_rows, model), F32, whole((ext_rows, model))),
         ((1, model), F32, whole((1, model))),
         ((8, 2 * NS), F32, whole((8, 2 * NS))),
         ((8, LANES), F32, whole((8, LANES)))],
        [pltpu.VMEM((ext_rows, bd), F32)], "last", 9, flags, *ins, after=state1,
    )

    stays1, stays2, d_norm = lax.optimization_barrier((state1[0], state1[2], d_norm))
    state1 = (stays1, state1[1], stays2, state1[3])

    d_skip_all = sums[1].reshape(members, group_heads, HEAD).sum(axis=2)

    def by_member(v, wide):
        return v.reshape(v.shape[0], members, wide).transpose(1, 0, 2).reshape(members, -1)

    small_grads = jnp.concatenate(
        [by_member(dtaps[:CONV], width), by_member(dtaps[CONV : CONV + 1], width),
         by_member(sums[0:1], width), by_member(dtaps_bc[:CONV], bc_cols),
         by_member(dtaps_bc[CONV : CONV + 1], bc_cols),
         ddt[0, :heads].reshape(members, -1), ddt[1, :heads].reshape(members, -1), d_skip_all],
        axis=1,
    )
    small_grads = jnp.pad(
        small_grads, ((0, 0), (0, small_rows * model - small_grads.shape[1]))
    ).reshape(members, small_rows, model)
    extra = jnp.concatenate(
        [dw_bd[: 2 * NS].reshape(members, bc_cols, model),
         dw_bd[2 * NS : 2 * NS + heads].reshape(members, group_heads, model),
         small_grads.astype(BF16),
         jnp.broadcast_to(gain_part[None], (members, 1, model)).astype(BF16)], axis=1,
    )
    extra = jnp.pad(extra, ((0, 0), (0, -extra.shape[1] % 16), (0, 0)))
    run3 = reduce_small(extra.reshape(members // 2, 2, -1, model))
    states = in_step([run1, run2, run3], [state1, state2, None])
    g1, g2, g3 = (jnp.concatenate(v, axis=0).astype(F32) for v in states)

    from_next = lax.ppermute(d_norm[:HALO], RC, back)
    d_normed = d_norm[HALO:]
    d_normed = jnp.concatenate(
        [d_normed[: tokens - HALO], d_normed[tokens - HALO :] + from_next], axis=0
    )
    x_rows = block_input.astype(F32)
    r_own = rstd[HALO:]
    d_v = d_normed * gain_in
    d_x = (
        d_out.astype(F32) + r_own * d_v
        - x_rows * r_own**3 * jnp.mean(d_v * x_rows, axis=1, keepdims=True)
    )
    flat = g3[side : side + small_rows].reshape(-1)
    s = [flat[cuts[i] : cuts[i + 1]] for i in range(len(sizes))]
    return (
        block_out,
        d_x,
        g3[side + small_rows],
        g2[:width].T,
        g1,
        g3[:bc_cols].T,
        g3[bc_cols:side].T,
        s[0].reshape(CONV, width),
        s[1],
        s[3].reshape(CONV, bc_cols),
        s[4],
        s[5],
        s[6],
        s[7],
        s[2],
        g2[width:],
    )


def solution(mesh):
    placed = (
        P(("dp", "row", "col"), None),
        P(("dp", "row", "col"), None),
        P("dp", None),
        P(),
        P(None, ("row", "col")),
        P(None, ("row", "col")),
        P(None, ("row", "col")),
        P(None, ("row", "col")),
        P(None, ("row", "col")),
        P(("row", "col")),
        P(None, ("row", "col")),
        P(("row", "col")),
        P(("row", "col")),
        P(("row", "col")),
        P(("row", "col")),
        P(("row", "col")),
        P(("row", "col"), None),
    )
    return jax.shard_map(
        on_device,
        mesh=mesh,
        in_specs=placed,
        out_specs=(
            P(("dp", "row", "col"), None),
            P(("dp", "row", "col"), None),
            P(),
            P(None, ("row", "col")),
            P(None, ("row", "col")),
            P(None, ("row", "col")),
            P(None, ("row", "col")),
            P(None, ("row", "col")),
            P(("row", "col")),
            P(None, ("row", "col")),
            P(("row", "col")),
            P(("row", "col")),
            P(("row", "col")),
            P(("row", "col")),
            P(("row", "col")),
            P(("row", "col"), None),
        ),
        check_vma=False,
    )
```
